256 devices in a mesh: dp: 8 (over y, core), mp: 32 (over z, x).
Axes of the slice: x: 4, y: 4, z: 8, core: 2. Of those that a mesh axis runs over, the one named last changes fastest.
Arguments:
- gradient: bfloat16 [12288, 28672], P('dp', 'mp'), as said below
- owners: int32 [32, 1], replicated, may hold values from 0 to 7, as said below
- left_old: float32 [24, 512, 512], P('dp', 'mp'), may hold values from -3 to 3
- right_old: float32 [48, 896, 896], P('dp', 'mp'), may hold values from -3 to 3
Outputs:
- left_stats: float32 [24, 512, 512], P('dp', 'mp')
- right_stats: float32 [48, 896, 896], P('dp', 'mp')
The draws below stay inside these ranges and needn't reach their ends.
Inputs may be any that keep to these rules, and one draw needn't show every extreme that they name: `owners`: each owner holds at most 6 and at least 2 blocks of the whole gradient; some owner holds exactly 6 and another exactly 2. `gradient`: finite values of order one or smaller.
All inputs are finite; a program needn't handle non-finite values.
Results may differ from the reference program's by a relative error of at most 0.0003.
Values sent between devices are 32-bit elements; how exact they have to be, the bound alone decides.
A program may use at most 64 MiB of HBM per device.

```python
import math
import jax
import jax.numpy as jnp
from jax import lax

M = 12288
N = 28672
BL = 512
RB = 896
NLB = 24
NB = 32
CAP = 6
N_DP = 8


def draw_gradient(key, part):
    key = jax.random.fold_in(key, 11)
    key_noise, key_rows, key_cols, key_left, key_right = jax.random.split(key, 5)
    noise = jax.random.normal(key_noise, (M, N), jnp.float32)
    lower, upper, shared = (0.5, 2.0, 0.6)
    row_scale = jnp.exp(jax.random.uniform(key_rows, (M, 1), jnp.float32, math.log(lower), math.log(upper)))
    col_scale = jnp.exp(jax.random.uniform(key_cols, (1, N), jnp.float32, math.log(0.5), math.log(2.0)))
    common = jax.random.normal(key_left, (M, 1), jnp.float32) * jax.random.normal(key_right, (1, N), jnp.float32)
    value = row_scale * col_scale * (noise + shared * common) * N ** (-0.5)
    return value.astype(jnp.bfloat16)


def draw_owners(key, part):
    key = jax.random.fold_in(key, 23)
    key_shift, key_order, key_perm = jax.random.split(key, 3)
    mean_count = NB // N_DP
    half_count = NB // (2 * N_DP)
    pair_count = N_DP // 2
    shifts = jax.random.randint(key_shift, (pair_count,), 0, half_count + 1, jnp.int32)
    pair_index = jnp.arange(pair_count, dtype=jnp.int32)
    shifts = jnp.where(pair_index == 0, half_count, shifts).astype(jnp.int32)
    counts = jnp.stack([mean_count + shifts, mean_count - shifts], axis=1).reshape(N_DP)
    ends = jnp.cumsum(counts).astype(jnp.int32)
    position = jnp.arange(NB, dtype=jnp.int32)
    slot_owner = jnp.sum((position[:, None] >= ends[None, :]).astype(jnp.int32), axis=1)
    order = jax.random.permutation(key_order, N_DP).astype(jnp.int32)
    shuffle = jax.random.permutation(key_perm, NB).astype(jnp.int32)
    owner_list = order[slot_owner[shuffle]]
    return owner_list.reshape(NB, 1).astype(jnp.int32)


def shard_levels(stream_key, dims, pieces, least, top_value):
    gain = 1.0
    for dim, blocks in pieces:
        steps = jax.random.uniform(jax.random.fold_in(jax.random.fold_in(stream_key, 6), dim), (blocks,), jnp.float32, least / len(pieces), top_value / len(pieces))
        gain = gain * jnp.repeat(jnp.exp(steps), dims[dim] // blocks).reshape((-1,) + (1,) * (len(dims) - 1 - dim))
    return gain


def gaussian(key, shape, deviation, limit, cuts=(), kind=jnp.bfloat16):
    result = jax.random.normal(key, shape, jnp.float32) * deviation
    if len(cuts) > 0:
        result = shard_levels(key, shape, cuts, -0.22, 0.18) * result
    return jnp.clip(result, min=-limit, max=limit).astype(kind)


def setup_inputs(seed: int = 0) -> dict:
    seeds = jax.random.split(jax.random.key(seed), 5)
    return {
        "gradient": draw_gradient(jax.random.fold_in(seeds[4], 71), 0),
        "owners": draw_owners(jax.random.fold_in(seeds[4], 71), 0),
        "left_old": gaussian(seeds[2], (NLB, BL, BL), 0.5, 3.0, ((0, 8), (1, 32)), jnp.float32),
        "right_old": gaussian(seeds[3], (N_DP * CAP, RB, RB), 0.5, 3.0, ((0, 8), (1, 32)), jnp.float32),
    }


BETA = 0.95


def block_gram(block_rows):
    return jnp.dot(block_rows, block_rows.T, preferred_element_type=jnp.float32)


def column_gram(block_cols):
    return jnp.dot(block_cols.T, block_cols, preferred_element_type=jnp.float32)


def reference(gradient, owners, left_old, right_old):
    left_blocks = gradient.reshape(NLB, BL, N)
    left_gram = lax.map(block_gram, left_blocks)
    left_stats = BETA * left_old + left_gram
    right_blocks = jnp.transpose(gradient.reshape(M, NB, RB), (1, 0, 2))
    right_gram = lax.map(column_gram, right_blocks)
    all_owners = owners[:, 0]
    same_owner = all_owners[:, None] == all_owners[None, :]
    block_range = jnp.arange(NB, dtype=jnp.int32)
    earlier = block_range[None, :] < block_range[:, None]
    owner_rank = jnp.sum((same_owner & earlier).astype(jnp.int32), axis=1)
    selector = ((all_owners[None, None, :] == jnp.arange(N_DP, dtype=jnp.int32)[:, None, None])
                & (owner_rank[None, None, :] == jnp.arange(CAP, dtype=jnp.int32)[None, :, None])).astype(jnp.float32)
    fresh_gram = jnp.einsum('okb,bad->okad', selector, right_gram, precision=lax.Precision.HIGHEST)
    valid = jnp.sum(selector, axis=2)
    old_slots = right_old.reshape(N_DP, CAP, RB, RB)
    right_stats = BETA * valid[:, :, None, None] * old_slots + fresh_gram
    return left_stats, right_stats.reshape(N_DP * CAP, RB, RB)
```

```python
import functools

import jax
import jax.numpy as jnp
from jax import lax
from jax.experimental import pallas as pl
from jax.experimental.pallas import tpu as pltpu
from jax.sharding import PartitionSpec as P

BETA = 0.95
F32 = jnp.float32
BF16 = jnp.bfloat16
RB = 896
T = 128
NT = 7
NMP = 32
NDP = 8
CAP = 6
RPM = 28
NY = 4
NX = 4
NZ = 8


def remote(src, dst, send_sem, recv_sem, dp, mp):
    return pltpu.make_async_remote_copy(
        src_ref=src,
        dst_ref=dst,
        send_sem=send_sem,
        recv_sem=recv_sem,
        device_id=(dp, mp),
        device_id_type=pl.DeviceIdType.MESH,
    )


def kernel(
    grad_ref, grad5_ref, table_ref, left_ref, right_ref,
    h, ht, a, part, ra, rb1, rb2, s2, r2, s3, r3,
    lp, lx1, lx2, lz, lzr, lt,
    in_sem, ra_send, ra_recv, rb_send, rb_recv, r2_send, r2_recv, r3_send, r3_recv,
    lx_send, lx_recv, lz_send, lz_recv, lt_sem,
):
    dp = lax.axis_index("dp")
    mp = lax.axis_index("mp")
    y, c = dp // 2, dp % 2
    z, x = mp // NX, mp % NX
    other = 1 - c

    load_h = pltpu.make_async_copy(grad_ref, h.at[:, pl.ds(0, RB)], in_sem.at[0])
    load_h.start()
    load_a = []
    for j in range(6):
        cp = pltpu.make_async_copy(grad5_ref.at[:, :, (x + j) % NX], a.at[j], in_sem.at[1 + j])
        cp.start()
        load_a.append(cp)

    barrier = pltpu.get_barrier_semaphore()

    def hello_mp(i, carry):
        pl.semaphore_signal(barrier, inc=1, device_id=(dp, (mp + i) % NMP), device_id_type=pl.DeviceIdType.MESH)
        return carry

    def hello_dp(i, carry):
        pl.semaphore_signal(barrier, inc=1, device_id=((dp + i) % NDP, mp), device_id_type=pl.DeviceIdType.MESH)
        return carry

    lax.fori_loop(1, NDP, hello_dp, 0)
    lax.fori_loop(1, NMP, hello_mp, 0)

    h[:, pl.ds(RB, T)] = jnp.zeros((h.shape[0], T), BF16)
    load_h.wait()
    for t in range(NT):
        ht[t * T:(t + 1) * T, :] = h[:, t * T:(t + 1) * T].T

    pl.semaphore_wait(barrier, NMP - 1 + NDP - 1)

    def has(q, core):
        return 2 * q + core < NT

    order = [(y + k) % NY for k in (2, 1, 3, 0)]

    def ra_copy(q, i):
        return remote(part.at[2 * q + other], ra.at[q], ra_send.at[i], ra_recv.at[i], dp + 1 - 2 * c, mp)

    for i, q in enumerate(order):
        cols = pl.ds(pl.multiple_of(q * 2 * T, 2 * T), 2 * T)
        block = jnp.dot(ht[...], h[:, cols], preferred_element_type=F32)
        part[2 * q] = block[:, :T]
        part[2 * q + 1] = block[:, T:]

        @pl.when(has(q, other))
        def _():
            ra_copy(q, i).start()

    for cp in load_a:
        cp.wait()

    def left_part(j):
        for l in range(3):
            rows = a[j, l].reshape(T, RB)
            cols = a[j:j + 3, l].reshape(3 * T, RB)
            lp[j, l] = lax.dot_general(rows, cols, (((1,), (1,)), ((), ())), preferred_element_type=F32)

    half = T // 2
    xr = z * NX + (x + 1) % NX
    xl = z * NX + (x + 3) % NX
    left_part(2)
    lx1_r = remote(lp.at[2, :, pl.ds(0, half)], lx1.at[0], lx_send.at[0], lx_recv.at[0], dp, xr)
    lx1_l = remote(lp.at[2, :, pl.ds(half, half)], lx1.at[1], lx_send.at[1], lx_recv.at[1], dp, xl)
    lx1_r.start()
    lx1_l.start()

    yr = 2 * ((y + 1) % NY) + c
    yl = 2 * ((y + 3) % NY) + c
    hr = RB // 2

    def ra_sum(i):
        q = order[i]

        @pl.when(has(q, c))
        def _():
            ra_copy(q, i).wait_recv()
            part[2 * q + c] = part[2 * q + c] + ra[q]

    q2, q1, q3, q0 = order
    ra_sum(0)
    rb1_r = remote(part.at[2 * q2 + c, pl.ds(0, hr)], rb1.at[0], rb_send.at[0], rb_recv.at[0], yr, mp)
    rb1_l = remote(part.at[2 * q2 + c, pl.ds(hr, hr)], rb1.at[1], rb_send.at[1], rb_recv.at[1], yl, mp)

    @pl.when(has(q2, c))
    def _():
        rb1_r.start()
        rb1_l.start()

    left_part(1)
    left_part(3)
    ra_sum(1)
    ra_sum(2)

    rb2_r = remote(part.at[2 * q1 + c], rb2.at[0], rb_send.at[2], rb_recv.at[2], yr, mp)
    rb2_l = remote(part.at[2 * q3 + c], rb2.at[1], rb_send.at[3], rb_recv.at[3], yl, mp)

    @pl.when(has(q1, c))
    def _():
        rb1_r.wait_recv()
        part[2 * q1 + c, :hr] = part[2 * q1 + c, :hr] + rb1[0]
        rb2_r.start()

    @pl.when(has(q3, c))
    def _():
        rb1_l.wait_recv()
        part[2 * q3 + c, hr:] = part[2 * q3 + c, hr:] + rb1[1]
        rb2_l.start()

    lx1_r.wait_recv()
    lp[1, :, :half] = lp[1, :, :half] + lx1[0]
    lx2_r = remote(lp.at[1], lx2.at[0], lx_send.at[2], lx_recv.at[2], dp, xr)
    lx2_r.start()
    lx1_l.wait_recv()
    lp[3, :, half:] = lp[3, :, half:] + lx1[1]
    lx2_l = remote(lp.at[3], lx2.at[1], lx_send.at[3], lx_recv.at[3], dp, xl)
    lx2_l.start()
    left_part(0)

    ra_sum(3)
    active = dp < NT

    def r2_copy(i):
        return remote(s2.at[(mp + i) % NMP], r2.at[NMP - i], r2_send, r2_recv, dp, (mp + i) % NMP)

    @pl.when(active)
    def _():
        rb2_r.wait_recv()
        rb2_l.wait_recv()
        part[dp] = part[dp] + rb2[0] + rb2[1]
        for m in range(NMP):
            s2[m] = part[dp, RPM * m:RPM * (m + 1)]

        def go(i, carry):
            r2_copy(i).start()
            return carry

        lax.fori_loop(1, NMP, go, 0)
        r2[0] = s2[mp]

    lx2_r.wait_recv()
    lx2_l.wait_recv()
    for l in range(3):
        band = lp[0, l] + lx2[0, l] + lx2[1, l]
        lz[:, l, :, :3 * T] = band.reshape(NZ, 16, 3 * T)
        lz[:, l, :, 3 * T:] = band[:, T:2 * T].T.reshape(NZ, 16, T)

    zr = ((z + 1) % NZ) * NX + x
    zl = ((z + NZ - 1) % NZ) * NX + x
    hc = 2 * T

    def lz_copies(s):
        to_r = (z + 5 - s) % NZ
        to_l = (z + NZ - 5 + s) % NZ
        if s == 1:
            src_r, dst_r = lz.at[to_r, :, :, pl.ds(0, hc)], lzr.at[0, 0, :, :, pl.ds(0, hc)]
            src_l, dst_l = lz.at[to_l, :, :, pl.ds(hc, hc)], lzr.at[1, 0, :, :, pl.ds(hc, hc)]
        else:
            src_r, dst_r = lz.at[to_r], lzr.at[0, s - 1]
            src_l, dst_l = lz.at[to_l], lzr.at[1, s - 1]
        return (
            remote(src_r, dst_r, lz_send.at[0, s - 1], lz_recv.at[0, s - 1], dp, zr),
            remote(src_l, dst_l, lz_send.at[1, s - 1], lz_recv.at[1, s - 1], dp, zl),
        )

    lz_all = [lz_copies(s) for s in (1, 2, 3, 4)]

    def lz_start(s):
        for cp in lz_all[s - 1]:
            cp.start()

    def lz_take(s):
        r, l = lz_all[s - 1]
        near = (z + 4 - s) % NZ
        r.wait_recv()
        if s == 1:
            lz[near, :, :, :hc] = lz[near, :, :, :hc] + lzr[0, 0, :, :, :hc]
        else:
            lz[near] = lz[near] + lzr[0, s - 1]
        far = (z + NZ - 4 + s) % NZ
        l.wait_recv()
        if s == 1:
            lz[far, :, :, hc:] = lz[far, :, :, hc:] + lzr[1, 0, :, :, hc:]
        else:
            lz[far] = lz[far] + lzr[1, s - 1]

    lz_start(1)
    lz_take(1)
    lz_start(2)

    def r3_copy(i):
        o = (dp + i) % NDP
        return remote(s3.at[o], r3.at[dp], r3_send.at[i], r3_recv.at[dp], o, mp)

    @pl.when(active)
    def _():
        everything = r2.at[pl.ds(1, NMP - 1)]
        pltpu.make_async_copy(everything, everything, r2_recv).wait()
        for o in range(NDP):
            for k in range(CAP):
                s3[o, RPM * k:RPM * (k + 1), :] = r2[table_ref[o * CAP + k]]
        for i in range(1, NDP):
            r3_copy(i).start()
        r3[dp] = s3[dp]

    for s in (2, 3):
        lz_take(s)
        lz_start(s + 1)
    lz_take(4)
    last = remote(lz.at[z, :, :, pl.ds(3 * T, T)], lt, lt_sem.at[0], lt_sem.at[1], dp, xr)
    last.start()

    p = lax.broadcasted_iota(jnp.int32, (NX * T, NX * T), 0)
    q = lax.broadcasted_iota(jnp.int32, (NX * T, NX * T), 1)
    place = ((p // 16) % NZ) * (16 * NX) + ((p // T + x) % NX) * 16 + p % 16
    perm = (place == q).astype(F32)
    last.wait_recv()
    for l in range(3):
        row = jnp.concatenate([lz[z, l, :, :3 * T], lt[l]], axis=1)
        left_ref[l] = jnp.dot(row, perm, precision=lax.Precision.HIGHEST, preferred_element_type=F32)

    for d in range(NT):
        @pl.when(dp != d)
        def _():
            pltpu.make_async_copy(r3.at[d], r3.at[d], r3_recv.at[d]).wait()

        for k in range(CAP):
            right_ref[k, :, d * T:(d + 1) * T] = r3[d, RPM * k:RPM * (k + 1), :]

    for i, q_ in enumerate(order):
        @pl.when(has(q_, other))
        def _():
            ra_copy(q_, i).wait_send()

    @pl.when(has(q2, c))
    def _():
        rb1_r.wait_send()
        rb1_l.wait_send()

    @pl.when(has(q1, c))
    def _():
        rb2_r.wait_send()

    @pl.when(has(q3, c))
    def _():
        rb2_l.wait_send()

    for cp in (lx1_r, lx1_l, lx2_r, lx2_l, last):
        cp.wait_send()
    for pair in lz_all:
        for cp in pair:
            cp.wait_send()

    @pl.when(active)
    def _():
        sent = s2.at[pl.ds(1, NMP - 1)]
        pltpu.make_async_copy(sent, sent, r2_send).wait()
        for i in range(1, NDP):
            r3_copy(i).wait_send()


def per_device(gradient, owners, left_old, right_old):
    rows = gradient.shape[0]
    all_owners = owners[:, 0]
    same_owner = all_owners[:, None] == all_owners[None, :]
    block = jnp.arange(NMP, dtype=jnp.int32)
    rank = jnp.sum((same_owner & (block[None, :] < block[:, None])).astype(jnp.int32), axis=1)
    place = all_owners * CAP + rank
    hit = place[None, :] == jnp.arange(NDP * CAP, dtype=jnp.int32)[:, None]
    source = jnp.sum(jnp.where(hit, block[None, :], 0), axis=1)
    table = (source - lax.axis_index("mp") + NMP) % NMP
    slot = jnp.arange(CAP, dtype=jnp.int32) + lax.axis_index("dp") * CAP
    valid = jnp.any(place[None, :] == slot[:, None], axis=1)

    left_gram, right_gram = pl.pallas_call(
        kernel,
        out_shape=(
            jax.ShapeDtypeStruct((3, 16, 512), F32),
            jax.ShapeDtypeStruct((CAP, RPM, RB), F32),
        ),
        in_specs=[
            pl.BlockSpec(memory_space=pl.ANY),
            pl.BlockSpec(memory_space=pl.ANY),
            pl.BlockSpec(memory_space=pltpu.SMEM),
        ],
        out_specs=(
            pl.BlockSpec(memory_space=pltpu.VMEM),
            pl.BlockSpec(memory_space=pltpu.VMEM),
        ),
        scratch_shapes=[
            pltpu.VMEM((rows, 1024), BF16),
            pltpu.VMEM((RB, rows), BF16),
            pltpu.VMEM((6, 3, NZ, 16, RB), BF16),
            pltpu.VMEM((8, RB, T), F32),
            pltpu.VMEM((NY, RB, T), F32),
            pltpu.VMEM((2, RB // 2, T), F32),
            pltpu.VMEM((2, RB, T), F32),
            pltpu.VMEM((NMP, RPM, T), F32),
            pltpu.VMEM((NMP, RPM, T), F32),
            pltpu.VMEM((NDP, CAP * RPM, T), F32),
            pltpu.VMEM((NDP, CAP * RPM, T), F32),
            pltpu.VMEM((NX, 3, T, 3 * T), F32),
            pltpu.VMEM((2, 3, T // 2, 3 * T), F32),
            pltpu.VMEM((2, 3, T, 3 * T), F32),
            pltpu.VMEM((NZ, 3, 16, 4 * T), F32),
            pltpu.VMEM((2, 4, 3, 16, 4 * T), F32),
            pltpu.VMEM((3, 16, T), F32),
            pltpu.SemaphoreType.DMA((7,)),
            pltpu.SemaphoreType.DMA((NY,)),
            pltpu.SemaphoreType.DMA((NY,)),
            pltpu.SemaphoreType.DMA((4,)),
            pltpu.SemaphoreType.DMA((4,)),
            pltpu.SemaphoreType.DMA,
            pltpu.SemaphoreType.DMA,
            pltpu.SemaphoreType.DMA((NDP,)),
            pltpu.SemaphoreType.DMA((NDP,)),
            pltpu.SemaphoreType.DMA((4,)),
            pltpu.SemaphoreType.DMA((4,)),
            pltpu.SemaphoreType.DMA((2, 4)),
            pltpu.SemaphoreType.DMA((2, 4)),
            pltpu.SemaphoreType.DMA((2,)),
        ],
        compiler_params=pltpu.CompilerParams(
            collective_id=0, has_side_effects=True, vmem_limit_bytes=48 * 1024 * 1024
        ),
        name="stats",
    )(gradient, gradient.reshape(3, NZ, NX, 16, RB), table)
    left_stats = BETA * left_old + left_gram
    right_stats = jnp.where(valid[:, None, None], BETA * right_old + right_gram, 0.0)
    return left_stats, right_stats


def solution(mesh):
    in_specs = (P("dp", "mp"), P(), P("dp", "mp", None), P("dp", "mp", None))
    out_specs = (P("dp", "mp", None), P("dp", "mp", None))
    return jax.shard_map(
        per_device, mesh=mesh, in_specs=in_specs, out_specs=out_specs, check_vma=False
    )
```

```python
import functools

import jax
import jax.numpy as jnp
from jax import lax
from jax.experimental import pallas as pl
from jax.experimental.pallas import tpu as pltpu
from jax.sharding import PartitionSpec as P

BETA = 0.95
F32 = jnp.float32
BF16 = jnp.bfloat16
RB = 896
T = 128
NT = 7
NMP = 32
NDP = 8
CAP = 6
RPM = 28
NY = 4
NX = 4
NZ = 8


def remote(src, dst, send_sem, recv_sem, dp, mp):
    return pltpu.make_async_remote_copy(
        src_ref=src,
        dst_ref=dst,
        send_sem=send_sem,
        recv_sem=recv_sem,
        device_id=(dp, mp),
        device_id_type=pl.DeviceIdType.MESH,
    )


def kernel(
    grad_ref, grad5_ref, owners_ref, left_ref, right_ref, scale_ref,
    h, a, pb, part, ra, rb1, rb2, r2a, r2b, s3a, s3b, r3a, r3b,
    lp, lx1, lx2, lz, rly, rlyh, fin, fint, perm, tabv, tab,
    in_sem, tab_sem, ra_send, ra_recv, rb1_send, rb1_recv, rb2_send, rb2_recv,
    r2_send, r2_recv, r3_send, r3_recv,
    lx1_send, lx1_recv, lx2_send, lx2_recv, lz_send, lz_recv,
):
    dp = lax.axis_index("dp")
    mp = lax.axis_index("mp")
    y, c = dp // 2, dp % 2
    z, x = mp // NX, mp % NX
    other = 1 - c
    half = T // 2
    xr = z * NX + (x + 1) % NX
    xl = z * NX + (x + 3) % NX
    yr = 2 * ((y + 1) % NY) + c
    yl = 2 * ((y + 3) % NY) + c
    active = dp < NT

    def has(q, core):
        return 2 * q + core < NT

    load_h = pltpu.make_async_copy(grad_ref, h.at[:, pl.ds(0, RB)], in_sem.at[0])
    load_h.start()
    load_a = {}
    for j in (2, 3, 4, 1, 5, 0):
        load_a[j] = pltpu.make_async_copy(grad5_ref.at[:, :, (x + j) % NX], a.at[j], in_sem.at[1 + j])
        load_a[j].start()

    barrier = pltpu.get_barrier_semaphore()

    def hello_mp(i, carry):
        pl.semaphore_signal(barrier, inc=1, device_id=(dp, (mp + i) % NMP), device_id_type=pl.DeviceIdType.MESH)
        return carry

    def hello_dp(i, carry):
        pl.semaphore_signal(barrier, inc=1, device_id=((dp + i) % NDP, mp), device_id_type=pl.DeviceIdType.MESH)
        return carry

    lax.fori_loop(1, NDP, hello_dp, 0)
    lax.fori_loop(1, NMP, hello_mp, 0)

    h[:, pl.ds(RB, T)] = jnp.zeros((h.shape[0], T), BF16)
    order = [(y + k) % NY for k in (2, 1, 3, 0)]
    q2, q1, q3, q0 = order

    def right_part(q):
        cols = pl.ds(pl.multiple_of(q * 2 * T, 2 * T), 2 * T)
        block = lax.dot_general(h[:, :RB], h[:, cols], (((0,), (0,)), ((), ())), preferred_element_type=F32)
        for e in range(2):
            pb[e] = block[:, e * T:(e + 1) * T]
            for m in range(NMP):
                part[2 * q + e, m] = pb[e, RPM * m:RPM * (m + 1)]

    def ra_copy(i):
        q = order[i]
        return remote(part.at[2 * q + other], ra.at[q], ra_send.at[i], ra_recv.at[i], dp + 1 - 2 * c, mp)

    def ra_go(i):
        @pl.when(has(order[i], other))
        def _():
            ra_copy(i).start()

    def ra_sum(i):
        q = order[i]

        @pl.when(has(q, c))
        def _():
            ra_copy(i).wait_recv()
            part[2 * q + c] = part[2 * q + c] + ra[q]

    def left_part(j):
        for l in range(3):
            rows = a[j, l].reshape(T, RB)
            cols = a[j:j + 3, l].reshape(3 * T, RB)
            lp[j, l] = lax.dot_general(rows, cols, (((1,), (1,)), ((), ())), preferred_element_type=F32)

    lx1_r = [remote(lp.at[2, l, pl.ds(0, half)], lx1.at[l, 0], lx1_send.at[l, 0], lx1_recv.at[l, 0], dp, xr) for l in range(3)]
    lx1_l = [remote(lp.at[2, l, pl.ds(half, half)], lx1.at[l, 1], lx1_send.at[l, 1], lx1_recv.at[l, 1], dp, xl) for l in range(3)]
    lx2_r = [remote(lp.at[1, l], lx2.at[l, 0], lx2_send.at[l, 0], lx2_recv.at[l, 0], dp, xr) for l in range(3)]
    lx2_l = [remote(lp.at[3, l], lx2.at[l, 1], lx2_send.at[l, 1], lx2_recv.at[l, 1], dp, xl) for l in range(3)]

    chunk = ((0, 16), (16, 12))
    hm = NMP // 2

    def rb1_copy(k, way):
        lo, n = chunk[k]
        src = part.at[2 * q2 + c, pl.ds(way * hm, hm), pl.ds(lo, n)]
        return remote(src, rb1.at[way, :, pl.ds(lo, n)], rb1_send.at[k, way], rb1_recv.at[k, way], (yr, yl)[way], mp)

    def rb2_copy(k, way):
        lo, n = chunk[k]
        src = part.at[2 * (q1, q3)[way] + c, :, pl.ds(lo, n)]
        return remote(src, rb2.at[way, :, pl.ds(lo, n)], rb2_send.at[k, way], rb2_recv.at[k, way], (yr, yl)[way], mp)

    def rb1_go():
        @pl.when(has(q2, c))
        def _():
            for k in range(2):
                for way in range(2):
                    rb1_copy(k, way).start()

    def rb2_go(k):
        lo, n = chunk[k]
        for way in range(2):
            q = (q1, q3)[way]

            @pl.when(has(q, c))
            def _():
                rb1_copy(k, way).wait_recv()
                t = 2 * q + c
                ms = slice(way * hm, (way + 1) * hm)
                part[t, ms, lo:lo + n] = part[t, ms, lo:lo + n] + rb1[way, :, lo:lo + n]
                rb2_copy(k, way).start()

    def lx2_go(l):
        lx1_r[l].wait_recv()
        lp[1, l, :half] = lp[1, l, :half] + lx1[l, 0]
        lx2_r[l].start()
        lx1_l[l].wait_recv()
        lp[3, l, half:] = lp[3, l, half:] + lx1[l, 1]
        lx2_l[l].start()

    def r2_go(k):
        lo, n = chunk[k]
        r2 = (r2a, r2b)[k]

        @pl.when(active)
        def _():
            for way in range(2):
                rb2_copy(k, way).wait_recv()
            part[dp, :, lo:lo + n] = part[dp, :, lo:lo + n] + rb2[0, :, lo:lo + n] + rb2[1, :, lo:lo + n]

            def go(i, carry):
                to = (mp + i) % NMP
                remote(
                    part.at[dp, to, pl.ds(lo, n)], r2.at[NMP - i],
                    r2_send.at[k], r2_recv.at[k], dp, to,
                ).start()
                return carry

            lax.fori_loop(1, NMP, go, 0)
            r2[0] = part[dp, mp, lo:lo + n]

    def r3_copy(k, i):
        o = (dp + i) % NDP
        s3, r3 = ((s3a, r3a), (s3b, r3b))[k]
        return remote(s3.at[o], r3.at[dp], r3_send.at[k, i], r3_recv.at[k, dp], o, mp)

    def r3_go(k):
        lo, n = chunk[k]
        s3, r3 = ((s3a, r3a), (s3b, r3b))[k]
        r2 = (r2a, r2b)[k]

        @pl.when(active)
        def _():
            everything = r2.at[pl.ds(1, NMP - 1)]
            pltpu.make_async_copy(everything, everything, r2_recv.at[k]).wait()
            for o in range(NDP):
                for s in range(CAP):
                    s3[o, n * s:n * (s + 1), :] = r2[tab[0, o * CAP + s]]
            for i in range(1, NDP):
                r3_copy(k, i).start()
            r3[dp] = s3[dp]

    def zz(k):
        return (z + NZ + k) % NZ

    def lz_copy(l, i):
        to, src, dst, dx = {
            0: (1, lz.at[l, zz(3)], rly.at[l, 0], 0),
            1: (-1, lz.at[l, zz(-3)], rly.at[l, 1], 0),
            2: (2, lz.at[l, zz(4), :, pl.ds(0, 2 * T)], rlyh.at[l, 0], 0),
            3: (-2, lz.at[l, zz(4), :, pl.ds(2 * T, 2 * T)], rlyh.at[l, 1], 0),
            4: (1, lz.at[l, zz(1), :, pl.ds(0, 3 * T)], fin.at[l, 0], 0),
            5: (-1, lz.at[l, zz(-1), :, pl.ds(0, 3 * T)], fin.at[l, 1], 0),
            6: (2, lz.at[l, zz(2), :, pl.ds(0, 3 * T)], fin.at[l, 2], 0),
            7: (-2, lz.at[l, zz(-2), :, pl.ds(0, 3 * T)], fin.at[l, 3], 0),
            8: (1, lz.at[l, zz(1), :, pl.ds(3 * T, T)], fint.at[l, 0], 1),
            9: (-1, lz.at[l, zz(-1), :, pl.ds(3 * T, T)], fint.at[l, 1], 1),
            10: (2, lz.at[l, zz(2), :, pl.ds(3 * T, T)], fint.at[l, 2], 1),
            11: (-2, lz.at[l, zz(-2), :, pl.ds(3 * T, T)], fint.at[l, 3], 1),
            12: (0, lz.at[l, z, :, pl.ds(3 * T, T)], fint.at[l, 4], 1),
        }[i]
        return remote(src, dst, lz_send.at[l, i], lz_recv.at[l, i], dp, zz(to) * NX + (x + dx) % NX)

    def lz_first(l):
        lx2_r[l].wait_recv()
        lx2_l[l].wait_recv()
        band = lp[0, l] + lx2[l, 0] + lx2[l, 1]
        lz[l, :, :, :3 * T] = band.reshape(NZ, 16, 3 * T)
        lz[l, :, :, 3 * T:] = band[:, T:2 * T].T.reshape(NZ, 16, T)
        for i in (2, 3, 0, 1, 4, 5, 8, 9, 12):
            lz_copy(l, i).start()

    def lz_second(l):
        for way in range(2):
            t = (zz(2), zz(-2))[way]
            lz_copy(l, way).wait_recv()
            lz_copy(l, 2 + way).wait_recv()
            cs = slice(way * 2 * T, (way + 1) * 2 * T)
            lz[l, t] = lz[l, t] + rly[l, way]
            lz[l, t, :, cs] = lz[l, t, :, cs] + rlyh[l, way]
            lz_copy(l, 6 + way).start()
            lz_copy(l, 10 + way).start()

    def lz_last(l):
        for i in range(4, 13):
            lz_copy(l, i).wait_recv()
        own = lz[l, z, :, :3 * T] + fin[l, 0] + fin[l, 1] + fin[l, 2] + fin[l, 3]
        turned = fint[l, 0] + fint[l, 1] + fint[l, 2] + fint[l, 3] + fint[l, 4]
        row = jnp.concatenate([own, turned], axis=1)
        total = None
        for _ in range(3):
            piece = row.astype(BF16)
            row = row - piece.astype(F32)
            term = jnp.dot(piece, perm[...], preferred_element_type=F32)
            total = term if total is None else total + term
        left_ref[l] = total

    def make_perm():
        p = lax.broadcasted_iota(jnp.int32, (NX * T, NX * T), 0)
        q = lax.broadcasted_iota(jnp.int32, (NX * T, NX * T), 1)
        place = ((p // 16) % NZ) * (16 * NX) + ((p // T + x) % NX) * 16 + p % 16
        perm[...] = (place == q).astype(F32).astype(BF16)

    def make_table():
        lane = lax.broadcasted_iota(jnp.int32, (8, T), 1)
        lane_owner = (lane * 43) >> 8
        lane_rank = lane - lane_owner * CAP
        seen = jnp.zeros((8, T), jnp.int32)
        found = jnp.zeros((8, T), jnp.int32)
        mine = jnp.int32(0)
        for b in range(NMP):
            o = owners_ref[0, b]
            same = lane_owner == o
            found = jnp.where(same & (seen == lane_rank), b, found)
            seen = seen + same.astype(jnp.int32)
            mine = mine + (o == dp).astype(jnp.int32)
        tabv[...] = (found - mp + NMP) % NMP
        cp = pltpu.make_async_copy(tabv, tab, tab_sem)
        cp.start()
        cp.wait()
        return [(k < mine).astype(F32) for k in range(CAP)]

    def right_out(k, valid):
        lo, n = chunk[k]
        r3 = (r3a, r3b)[k]
        for d in range(NT):
            @pl.when(dp != d)
            def _():
                pltpu.make_async_copy(r3.at[d], r3.at[d], r3_recv.at[k, d]).wait()

            for s in range(CAP):
                right_ref[s, lo:lo + n, d * T:(d + 1) * T] = r3[d, n * s:n * (s + 1), :] * valid[s]

    load_h.wait()
    right_part(q2)
    for j in (2, 3, 4):
        load_a[j].wait()
    left_part(2)
    pl.semaphore_wait(barrier, NMP - 1 + NDP - 1)
    ra_go(0)
    for l in range(3):
        lx1_r[l].start()
        lx1_l[l].start()
    right_part(q1)
    ra_go(1)
    right_part(q3)
    ra_go(2)
    ra_sum(0)
    rb1_go()
    right_part(q0)
    ra_go(3)
    for j in (1, 5, 0):
        load_a[j].wait()
    left_part(1)
    left_part(3)
    lx2_go(0)
    ra_sum(1)
    ra_sum(2)
    rb2_go(0)
    lx2_go(1)
    lx2_go(2)
    rb2_go(1)
    left_part(0)
    ra_sum(3)
    valid = make_table()
    make_perm()
    scale_ref[...] = jnp.stack([jnp.full((T,), BETA * v, F32) for v in valid] + [jnp.zeros((T,), F32)] * 2)
    lz_first(0)
    r2_go(0)
    lz_second(0)
    lz_first(1)
    r2_go(1)
    lz_second(1)
    lz_first(2)
    r3_go(0)
    lz_second(2)
    r3_go(1)
    for l in range(3):
        lz_last(l)
    right_out(0, valid)
    right_out(1, valid)

    for i in range(NY):
        @pl.when(has(order[i], other))
        def _():
            ra_copy(i).wait_send()

    @pl.when(has(q2, c))
    def _():
        for k in range(2):
            for way in range(2):
                rb1_copy(k, way).wait_send()

    for way in range(2):
        @pl.when(has((q1, q3)[way], c))
        def _():
            for k in range(2):
                rb2_copy(k, way).wait_send()

    for l in range(3):
        for cp in (lx1_r[l], lx1_l[l], lx2_r[l], lx2_l[l]):
            cp.wait_send()
        for i in range(13):
            lz_copy(l, i).wait_send()

    @pl.when(active)
    def _():
        for k in range(2):
            sent = (r2a, r2b)[k].at[pl.ds(1, NMP - 1)]
            pltpu.make_async_copy(sent, sent, r2_send.at[k]).wait()
            for i in range(1, NDP):
                r3_copy(k, i).wait_send()


def per_device(gradient, owners, left_old, right_old):
    rows = gradient.shape[0]
    dma = pltpu.SemaphoreType.DMA
    left_gram, right_gram, scale = pl.pallas_call(
        kernel,
        out_shape=(
            jax.ShapeDtypeStruct((3, 16, 512), F32),
            jax.ShapeDtypeStruct((CAP, RPM, RB), F32),
            jax.ShapeDtypeStruct((8, T), F32),
        ),
        in_specs=[
            pl.BlockSpec(memory_space=pltpu.HBM),
            pl.BlockSpec(memory_space=pltpu.HBM),
            pl.BlockSpec(memory_space=pltpu.SMEM),
        ],
        out_specs=(pl.BlockSpec(memory_space=pltpu.VMEM),) * 3,
        scratch_shapes=[
            pltpu.VMEM((rows, 1024), BF16),
            pltpu.VMEM((6, 3, NZ, 16, RB), BF16),
            pltpu.VMEM((2, RB, T), F32),
            pltpu.VMEM((8, NMP, RPM, T), F32),
            pltpu.VMEM((NY, NMP, RPM, T), F32),
            pltpu.VMEM((2, NMP // 2, RPM, T), F32),
            pltpu.VMEM((2, NMP, RPM, T), F32),
            pltpu.VMEM((NMP, 16, T), F32),
            pltpu.VMEM((NMP, 12, T), F32),
            pltpu.VMEM((NDP, CAP * 16, T), F32),
            pltpu.VMEM((NDP, CAP * 12, T), F32),
            pltpu.VMEM((NDP, CAP * 16, T), F32),
            pltpu.VMEM((NDP, CAP * 12, T), F32),
            pltpu.VMEM((NX, 3, T, 3 * T), F32),
            pltpu.VMEM((3, 2, T // 2, 3 * T), F32),
            pltpu.VMEM((3, 2, T, 3 * T), F32),
            pltpu.VMEM((3, NZ, 16, 4 * T), F32),
            pltpu.VMEM((3, 2, 16, 4 * T), F32),
            pltpu.VMEM((3, 2, 16, 2 * T), F32),
            pltpu.VMEM((3, 4, 16, 3 * T), F32),
            pltpu.VMEM((3, 5, 16, T), F32),
            pltpu.VMEM((4 * T, 4 * T), BF16),
            pltpu.VMEM((8, T), jnp.int32),
            pltpu.SMEM((8, T), jnp.int32),
            dma((7,)), dma,
            dma((NY,)), dma((NY,)),
            dma((2, 2)), dma((2, 2)), dma((2, 2)), dma((2, 2)),
            dma((2,)), dma((2,)), dma((2, NDP)), dma((2, NDP)),
            dma((3, 2)), dma((3, 2)), dma((3, 2)), dma((3, 2)),
            dma((3, 13)), dma((3, 13)),
        ],
        compiler_params=pltpu.CompilerParams(
            collective_id=0, has_side_effects=True, vmem_limit_bytes=56 * 1024 * 1024
        ),
        name="stats",
    )(gradient, gradient.reshape(3, NZ, NX, 16, RB), owners.reshape(1, NMP))
    left_stats = BETA * left_old + left_gram
    right_stats = scale[:CAP, :1, None] * right_old + right_gram
    return left_stats, right_stats


def solution(mesh):
    in_specs = (P("dp", "mp"), P(), P("dp", "mp", None), P("dp", "mp", None))
    out_specs = (P("dp", "mp", None), P("dp", "mp", None))
    return jax.shard_map(
        per_device, mesh=mesh, in_specs=in_specs, out_specs=out_specs, check_vma=False
    )
```

```python
import jax
import jax.numpy as jnp
from jax import lax
from jax.experimental import pallas as pl
from jax.experimental.pallas import tpu as pltpu
from jax.sharding import PartitionSpec as P

BETA = 0.95
F32 = jnp.float32
BF16 = jnp.bfloat16
RB = 896
T = 128
NT = 7
NMP = 32
NDP = 8
CAP = 6
RPM = 28
NY = 4
NX = 4
NZ = 8

CHUNK = ((0, 16), (16, 12))

LEFT_TILES = (
    ((0, 0), (2, 2), (1, 3)),
    ((0, 1), (2, 3)),
    ((1, 1), (3, 3), (2, 0)),
    ((0, 3), (2, 1)),
)


def remote(src, dst, send_sem, recv_sem, dp, mp):
    return pltpu.make_async_remote_copy(
        src_ref=src,
        dst_ref=dst,
        send_sem=send_sem,
        recv_sem=recv_sem,
        device_id=(dp, mp),
        device_id_type=pl.DeviceIdType.MESH,
    )


def kernel(
    grad_ref, grad5_ref, owners_ref, left_ref, right_ref, scale_ref,
    h, a, part, ra, rb1, rb2, tall, t28, r2a, r2b, s3a, s3b, r3a, r3b,
    lp, lx1, lx2, lz, rly, rlyh, fin, perm, tabv, tab,
    in_sem, tab_sem, ra_send, ra_recv, rb_send, rb_recv,
    r2_send, r2_recv, r3_send, r3_recv,
    lx_send, lx_recv, lz_send, lz_recv, fin_send, fin_recv,
):
    dp = lax.axis_index("dp")
    mp = lax.axis_index("mp")
    y, c = dp // 2, dp % 2
    z, x = mp // NX, mp % NX
    other = 1 - c
    half = T // 2
    xs = (z * NX + (x + 1) % NX, z * NX + (x + 3) % NX)
    ys = (2 * ((y + 1) % NY) + c, 2 * ((y + 3) % NY) + c)
    active = dp < NT

    def has(q, core):
        return 2 * q + core < NT

    rows = h.shape[0]
    load_h = []
    for i in range(4):
        n = rows // 4
        cp = pltpu.make_async_copy(grad_ref.at[pl.ds(i * n, n)], h.at[pl.ds(i * n, n)], in_sem.at[i])
        cp.start()
        load_h.append(cp)
    load_a = []
    for g in range(NX):
        cp = pltpu.make_async_copy(grad5_ref.at[:, :, g], a.at[:, g], in_sem.at[4 + g])
        cp.start()
        load_a.append(cp)

    barrier = pltpu.get_barrier_semaphore()

    def hello_mp(i, carry):
        pl.semaphore_signal(barrier, inc=1, device_id=(dp, (mp + i) % NMP), device_id_type=pl.DeviceIdType.MESH)
        return carry

    def hello_dp(i, carry):
        pl.semaphore_signal(barrier, inc=1, device_id=((dp + i) % NDP, mp), device_id_type=pl.DeviceIdType.MESH)
        return carry

    lax.fori_loop(1, NDP, hello_dp, 0)
    lax.fori_loop(1, NMP, hello_mp, 0)

    def right_part(q):
        lo = 2 * T * q
        wide = min(2 * T, RB - lo)
        block = lax.dot_general(
            h[:, lo:RB], h[:, lo:lo + wide], (((0,), (0,)), ((), ())), preferred_element_type=F32
        )
        for col in range(2 * q, 2 * q + wide // T):
            for row in range(col, NT):
                d = (row + col) % NT
                u = (4 * d) % NT
                k = min((row - u) % NT, (u - row) % NT)
                i, j = (row - 2 * q) * T, (col - 2 * q) * T
                part[d, k] = block[i:i + T, j:j + T]

    order = [(y + k) % NY for k in (2, 1, 3, 0)]
    q2, q1, q3, q0 = order

    def ra_copy(i):
        q = order[i]
        return remote(part.at[2 * q + other], ra.at[q], ra_send.at[i], ra_recv.at[i], dp + 1 - 2 * c, mp)

    def ra_go(i):
        @pl.when(has(order[i], other))
        def _():
            ra_copy(i).start()

    def rb_copy(step, way):
        i = 2 * step + way
        tiles = pl.ds(2 * way, 2) if step != 1 else pl.ds(2 - 2 * way, 2)
        q = (q2, (q1, q3)[way], (q1, q3)[way])[step]
        dst = rb1.at[way] if step == 0 else rb2.at[way, tiles]
        return remote(part.at[2 * q + c, tiles], dst, rb_send.at[i], rb_recv.at[i], ys[way], mp)

    def ra_sum(i):
        q = order[i]

        @pl.when(has(q, c))
        def _():
            ra_copy(i).wait_recv()
            part[2 * q + c] = part[2 * q + c] + ra[q]
            if i == 0:
                rb_copy(0, 0).start()
                rb_copy(0, 1).start()
            elif i < 3:
                rb_copy(1, i - 1).start()

    def rb_second():
        for way in range(2):
            q = (q1, q3)[way]

            @pl.when(has(q, c))
            def _():
                rb_copy(0, way).wait_recv()
                t = 2 * q + c
                part[t, 2 * way:2 * way + 2] = part[t, 2 * way:2 * way + 2] + rb1[way]
                rb_copy(2, way).start()

    def right_whole():
        @pl.when(active)
        def _():
            for way in range(2):
                rb_copy(1, way).wait_recv()
                rb_copy(2, way).wait_recv()
            u = (4 * dp) % NT
            for k in range(4):
                tile = part[dp, k] + rb2[0, k] + rb2[1, k]
                one = (u + k) % NT
                two = (u + NT - k) % NT
                if k == 0:
                    tall[pl.ds(pl.multiple_of(one * T, T), T), :] = tile
                else:
                    big = jnp.maximum(one, two)
                    small = jnp.minimum(one, two)
                    tall[pl.ds(pl.multiple_of(big * T, T), T), :] = tile
                    tall[pl.ds(pl.multiple_of(small * T, T), T), :] = tile.T
            for m in range(NMP):
                t28[m] = tall[RPM * m:RPM * (m + 1)]

    def r2_go(k):
        lo, n = CHUNK[k]
        r2 = (r2a, r2b)[k]

        @pl.when(active)
        def _():
            def go(i, carry):
                to = (mp + i) % NMP
                remote(t28.at[to, pl.ds(lo, n)], r2.at[NMP - i], r2_send.at[k], r2_recv.at[k], dp, to).start()
                return carry

            lax.fori_loop(1, NMP, go, 0)
            r2[0] = t28[mp, lo:lo + n]

    def r3_copy(k, i):
        o = (dp + i) % NDP
        s3, r3 = ((s3a, r3a), (s3b, r3b))[k]
        return remote(s3.at[o], r3.at[dp], r3_send.at[k, i], r3_recv.at[k, dp], o, mp)

    def r3_go(k):
        n = CHUNK[k][1]
        s3, r3 = ((s3a, r3a), (s3b, r3b))[k]
        r2 = (r2a, r2b)[k]

        @pl.when(active)
        def _():
            everything = r2.at[pl.ds(1, NMP - 1)]
            pltpu.make_async_copy(everything, everything, r2_recv.at[k]).wait()
            for o in range(NDP):
                for s in range(CAP):
                    s3[o, n * s:n * (s + 1), :] = r2[tab[0, o * CAP + s]]
            for i in range(1, NDP):
                r3_copy(k, i).start()
            r3[dp] = s3[dp]

    def left_part(l):
        g = a[l].reshape(NX * T, RB)
        block = lax.dot_general(g, g, (((1,), (1,)), ((), ())), preferred_element_type=F32)
        for v in range(4):
            for i, (r, s) in enumerate(LEFT_TILES[v]):
                lp[l, v, i] = block[r * T:(r + 1) * T, s * T:(s + 1) * T]

    def by_parity(value, fn):
        @pl.when(value % 2 == 0)
        def _():
            fn(3)

        @pl.when(value % 2 == 1)
        def _():
            fn(2)

    def lx_copy(l, step, way, n):
        i = 2 * step + way
        v = ((x + 2, x + 1, x + 1), (x + 2, x + 3, x + 3))[way][step]
        v = (v + 4 - l) % 4
        lo = half * way if step != 1 else half * (1 - way)
        tiles = pl.ds(0, n)
        part_rows = pl.ds(lo, half)
        dst = lx1.at[l, way, tiles] if step == 0 else lx2.at[l, way, tiles, part_rows]
        src = lp.at[l, v, tiles, part_rows]
        return remote(src, dst, lx_send.at[l, i], lx_recv.at[l, i], dp, xs[way])

    def lx_start(l, step):
        def go(n):
            lx_copy(l, step, 0, n).start()
            lx_copy(l, step, 1, n).start()

        by_parity(x + 4 - l + (0 if step == 0 else 1), go)

    def lx_second(l):
        def go(n):
            for way in range(2):
                lx_copy(l, 0, way, n).wait_recv()
                v = (x + (1, 3)[way] + 4 - l) % 4
                cut = slice(half * way, half * (way + 1))
                lp[l, v, :n, cut] = lp[l, v, :n, cut] + lx1[l, way, :n]
                lx_copy(l, 2, way, n).start()

        by_parity(x + 1 + 4 - l, go)

    def zz(k):
        return (z + NZ + k) % NZ

    def lz_copy(l, i):
        to, src, dst = (
            (1, lz.at[l, zz(3)], rly.at[l, 0]),
            (-1, lz.at[l, zz(-3)], rly.at[l, 1]),
            (2, lz.at[l, zz(4), pl.ds(0, 2)], rlyh.at[l, 0]),
            (-2, lz.at[l, zz(4), pl.ds(2, 2)], rlyh.at[l, 1]),
        )[i]
        return remote(src, dst, lz_send.at[l, i], lz_recv.at[l, i], dp, zz(to) * NX + x)

    hops = (0, 1, -1, 2, -2)

    def fin_start(l, j):
        for r in range(0 if j else 1, 4):
            g = (x + 4 - r) % 4
            to = zz(hops[j])
            remote(lz.at[l, to, g], fin.at[l, 4 * j + r], fin_send.at[l], fin_recv.at[l], dp, to * NX + g).start()

    def lz_first(l):
        def go(n):
            for way in range(2):
                lx_copy(l, 1, way, n).wait_recv()
                lx_copy(l, 2, way, n).wait_recv()
            v = (x + 4 - l) % 4
            tiles = [lp[l, v, i] + lx2[l, 0, i] + lx2[l, 1, i] for i in range(n)]

            def put(g, tile):
                lz[l, :, g] = tile.reshape(NZ, 16, T)

            if n == 3:
                w = v // 2
                put(w, tiles[0])
                put(w + 2, tiles[1])
                put(w + 1, tiles[2])
                put((w + 3) % 4, tiles[2].T)
            else:
                put(0, tiles[0])
                put(v, tiles[0].T)
                put(2, tiles[1])
                put((v + 2) % 4, tiles[1].T)

        by_parity(x + 4 - l, go)
        for i in (2, 3, 0, 1):
            lz_copy(l, i).start()
        for j in (1, 2, 0):
            fin_start(l, j)
        fin[l, 0] = lz[l, z, x]

    def lz_second(l):
        for way in range(2):
            t = (zz(2), zz(-2))[way]
            lz_copy(l, way).wait_recv()
            lz_copy(l, 2 + way).wait_recv()
            lz[l, t] = lz[l, t] + rly[l, way]
            lz[l, t, 2 * way:2 * way + 2] = lz[l, t, 2 * way:2 * way + 2] + rlyh[l, way]
            fin_start(l, 3 + way)

    def lz_last(l):
        everything = fin.at[l, pl.ds(1, 19)]
        pltpu.make_async_copy(everything, everything, fin_recv.at[l]).wait()
        row = []
        for g in range(4):
            r = (g + l) % 4
            row.append(fin[l, r] + fin[l, 4 + r] + fin[l, 8 + r] + fin[l, 12 + r] + fin[l, 16 + r])
        row = jnp.concatenate(row, axis=1)
        total = None
        for _ in range(3):
            piece = row.astype(BF16)
            row = row - piece.astype(F32)
            term = jnp.dot(piece, perm[...], preferred_element_type=F32)
            total = term if total is None else total + term
        left_ref[l] = total

    def make_perm():
        p = lax.broadcasted_iota(jnp.int32, (NX * T, NX * T), 0)
        q = lax.broadcasted_iota(jnp.int32, (NX * T, NX * T), 1)
        place = ((p // 16) % NZ) * (16 * NX) + (p // T) * 16 + p % 16
        perm[...] = (place == q).astype(F32).astype(BF16)

    def make_table():
        lane = lax.broadcasted_iota(jnp.int32, (8, T), 1)
        lane_owner = (lane * 43) >> 8
        lane_rank = lane - lane_owner * CAP
        seen = jnp.zeros((8, T), jnp.int32)
        found = jnp.zeros((8, T), jnp.int32)
        mine = jnp.int32(0)
        for b in range(NMP):
            o = owners_ref[0, b]
            same = lane_owner == o
            found = jnp.where(same & (seen == lane_rank), b, found)
            seen = seen + same.astype(jnp.int32)
            mine = mine + (o == dp).astype(jnp.int32)
        tabv[...] = (found - mp + NMP) % NMP
        cp = pltpu.make_async_copy(tabv, tab, tab_sem)
        cp.start()
        cp.wait()
        valid = [(k < mine).astype(F32) for k in range(CAP)]
        for k in range(CAP):
            scale_ref[k] = BETA * valid[k]
        return valid

    def right_out(k, valid):
        lo, n = CHUNK[k]
        r3 = (r3a, r3b)[k]
        for d in range(NT):
            @pl.when(dp != d)
            def _():
                pltpu.make_async_copy(r3.at[d], r3.at[d], r3_recv.at[k, d]).wait()

        first = (RPM * mp + lo) // T
        last = (RPM * mp + lo + n - 1) // T
        row = lax.broadcasted_iota(jnp.int32, (n, T), 0) + (RPM * mp + lo)
        upper = row < last * T
        for g in range(NT):
            one = (g + first) % NT
            two = (g + last) % NT
            for s in range(CAP):
                cut = slice(n * s, n * (s + 1))
                value = jnp.where(upper, r3[one, cut, :], r3[two, cut, :])
                right_ref[s, lo:lo + n, g * T:(g + 1) * T] = value * valid[s]

    for cp in load_h:
        cp.wait()
    for q in range(4):
        right_part(q)
    pl.semaphore_wait(barrier, NMP - 1 + NDP - 1)
    for i in range(4):
        ra_go(i)
    for cp in load_a:
        cp.wait()
    left_part(0)
    lx_start(0, 0)
    lx_start(0, 1)
    left_part(1)
    lx_start(1, 0)
    left_part(2)
    lx_start(2, 0)
    for i in range(4):
        ra_sum(i)
    valid = make_table()
    lx_second(0)
    lx_start(1, 1)
    rb_second()
    lx_second(1)
    lx_start(2, 1)
    lx_second(2)
    make_perm()
    lz_first(0)
    right_whole()
    r2_go(0)
    r2_go(1)
    lz_first(1)
    lz_second(0)
    lz_second(1)
    r3_go(0)
    lz_first(2)
    r3_go(1)
    lz_second(2)
    for l in range(3):
        lz_last(l)
    right_out(0, valid)
    right_out(1, valid)

    for i in range(NY):
        @pl.when(has(order[i], other))
        def _():
            ra_copy(i).wait_send()

    @pl.when(has(q2, c))
    def _():
        rb_copy(0, 0).wait_send()
        rb_copy(0, 1).wait_send()

    for way in range(2):
        @pl.when(has((q1, q3)[way], c))
        def _():
            rb_copy(1, way).wait_send()
            rb_copy(2, way).wait_send()

    for l in range(3):
        for step in range(3):
            def done(n):
                lx_copy(l, step, 0, n).wait_send()
                lx_copy(l, step, 1, n).wait_send()

            by_parity(x + 4 - l + (0 if step == 0 else 1), done)
        for i in range(4):
            lz_copy(l, i).wait_send()
        sent = fin.at[l, pl.ds(1, 19)]
        pltpu.make_async_copy(sent, sent, fin_send.at[l]).wait()

    @pl.when(active)
    def _():
        for k in range(2):
            sent = (r2a, r2b)[k].at[pl.ds(1, NMP - 1)]
            pltpu.make_async_copy(sent, sent, r2_send.at[k]).wait()
            for i in range(1, NDP):
                r3_copy(k, i).wait_send()


def per_device(gradient, owners, left_old, right_old):
    rows = gradient.shape[0]
    dma = pltpu.SemaphoreType.DMA
    na, nb = CHUNK[0][1], CHUNK[1][1]
    left_gram, right_gram, scale = pl.pallas_call(
        kernel,
        out_shape=(
            jax.ShapeDtypeStruct((3, 16, 512), F32),
            jax.ShapeDtypeStruct((CAP, RPM, RB), F32),
            jax.ShapeDtypeStruct((CAP,), F32),
        ),
        in_specs=[
            pl.BlockSpec(memory_space=pl.ANY),
            pl.BlockSpec(memory_space=pl.ANY),
            pl.BlockSpec(memory_space=pltpu.SMEM),
        ],
        out_specs=(
            pl.BlockSpec(memory_space=pltpu.VMEM),
            pl.BlockSpec(memory_space=pltpu.VMEM),
            pl.BlockSpec(memory_space=pltpu.SMEM),
        ),
        scratch_shapes=[
            pltpu.VMEM((rows, RB), BF16),
            pltpu.VMEM((3, NX, NZ, 16, RB), BF16),
            pltpu.VMEM((NDP, 4, T, T), F32),
            pltpu.VMEM((NY, 4, T, T), F32),
            pltpu.VMEM((2, 2, T, T), F32),
            pltpu.VMEM((2, 4, T, T), F32),
            pltpu.VMEM((RB, T), F32),
            pltpu.VMEM((NMP, RPM, T), F32),
            pltpu.VMEM((NMP, na, T), F32),
            pltpu.VMEM((NMP, nb, T), F32),
            pltpu.VMEM((NDP, CAP * na, T), F32),
            pltpu.VMEM((NDP, CAP * nb, T), F32),
            pltpu.VMEM((NDP, CAP * na, T), F32),
            pltpu.VMEM((NDP, CAP * nb, T), F32),
            pltpu.VMEM((3, 4, 3, T, T), F32),
            pltpu.VMEM((3, 2, 3, T // 2, T), F32),
            pltpu.VMEM((3, 2, 3, T, T), F32),
            pltpu.VMEM((3, NZ, 4, 16, T), F32),
            pltpu.VMEM((3, 2, 4, 16, T), F32),
            pltpu.VMEM((3, 2, 2, 16, T), F32),
            pltpu.VMEM((3, 20, 16, T), F32),
            pltpu.VMEM((4 * T, 4 * T), BF16),
            pltpu.VMEM((8, T), jnp.int32),
            pltpu.SMEM((8, T), jnp.int32),
            dma((8,)), dma,
            dma((NY,)), dma((NY,)), dma((6,)), dma((6,)),
            dma((2,)), dma((2,)), dma((2, NDP)), dma((2, NDP)),
            dma((3, 6)), dma((3, 6)), dma((3, 4)), dma((3, 4)), dma((3,)), dma((3,)),
        ],
        compiler_params=pltpu.CompilerParams(
            collective_id=0, has_side_effects=True, vmem_limit_bytes=105 * 512 * 1024
        ),
        name="stats",
    )(gradient, gradient.reshape(3, NZ, NX, 16, RB), owners.reshape(1, NMP))
    left_stats = BETA * left_old + left_gram
    right_stats = scale[:, None, None] * right_old + right_gram
    return left_stats, right_stats


def solution(mesh):
    in_specs = (P("dp", "mp"), P(), P("dp", "mp", None), P("dp", "mp", None))
    out_specs = (P("dp", "mp", None), P("dp", "mp", None))
    return jax.shard_map(
        per_device, mesh=mesh, in_specs=in_specs, out_specs=out_specs, check_vma=False
    )
```

```python
import jax
import jax.numpy as jnp
from jax import lax
from jax.experimental import pallas as pl
from jax.experimental.pallas import tpu as pltpu
from jax.sharding import PartitionSpec as P

BETA = 0.95
F32 = jnp.float32
BF16 = jnp.bfloat16
RB = 896
T = 128
NT = 7
NMP = 32
NDP = 8
CAP = 6
RPM = 28
NY = 4
NX = 4
NZ = 8

CHUNK = ((0, 16), (16, 12))

LEFT_TILES = (
    ((0, 0), (2, 2), (1, 3)),
    ((0, 1), (2, 3)),
    ((1, 1), (3, 3), (2, 0)),
    ((0, 3), (2, 1)),
)


def remote(src, dst, send_sem, recv_sem, dp, mp):
    return pltpu.make_async_remote_copy(
        src_ref=src,
        dst_ref=dst,
        send_sem=send_sem,
        recv_sem=recv_sem,
        device_id=(dp, mp),
        device_id_type=pl.DeviceIdType.MESH,
    )


def kernel(
    grad_ref, owners_ref, left_ref, right_ref, scale_ref,
    h, a, part, ra, rb1, rb2, tall, t28, r2a, r2b, s3a, s3b, r3a, r3b,
    lp, lx1, lx2, lz, rly, rlyh, fin, zg, zr1, zr2, zx, perm, tabv, tab,
    in_sem, tab_sem, ra_send, ra_recv, rb_send, rb_recv,
    r2_send, r2_recv, r3_send, r3_recv,
    lx_send, lx_recv, lz_send, lz_recv, fin_send, fin_recv,
    zr_send, zr_recv, zx_send, zx_recv,
):
    dp = lax.axis_index("dp")
    mp = lax.axis_index("mp")
    y, c = dp // 2, dp % 2
    z, x = mp // NX, mp % NX
    other = 1 - c
    half = T // 2
    xs = (z * NX + (x + 1) % NX, z * NX + (x + 3) % NX)
    ys = (2 * ((y + 1) % NY) + c, 2 * ((y + 3) % NY) + c)
    active = dp < NT

    def has(q, core):
        return 2 * q + core < NT

    rows = h.shape[0]
    load_h = []
    for i in range(4):
        n = rows // 4
        cp = pltpu.make_async_copy(grad_ref.at[pl.ds(i * n, n)], h.at[pl.ds(i * n, n)], in_sem.at[i])
        cp.start()
        load_h.append(cp)

    barrier = pltpu.get_barrier_semaphore()

    def hello_mp(i, carry):
        pl.semaphore_signal(barrier, inc=1, device_id=(dp, (mp + i) % NMP), device_id_type=pl.DeviceIdType.MESH)
        return carry

    def hello_dp(i, carry):
        pl.semaphore_signal(barrier, inc=1, device_id=((dp + i) % NDP, mp), device_id_type=pl.DeviceIdType.MESH)
        return carry

    lax.fori_loop(1, NDP, hello_dp, 0)
    lax.fori_loop(1, NMP, hello_mp, 0)

    def right_part(q):
        lo = 2 * T * q
        wide = min(2 * T, RB - lo)
        block = lax.dot_general(
            h[:, lo:RB], h[:, lo:lo + wide], (((0,), (0,)), ((), ())), preferred_element_type=F32
        )
        for col in range(2 * q, 2 * q + wide // T):
            for row in range(col, NT):
                d = (row + col) % NT
                u = (4 * d) % NT
                k = min((row - u) % NT, (u - row) % NT)
                i, j = (row - 2 * q) * T, (col - 2 * q) * T
                part[d, k] = block[i:i + T, j:j + T]

    order = [(y + k) % NY for k in (2, 1, 3, 0)]
    q2, q1, q3, q0 = order

    def ra_copy(i):
        q = order[i]
        return remote(part.at[2 * q + other], ra.at[q], ra_send.at[i], ra_recv.at[i], dp + 1 - 2 * c, mp)

    def ra_go(i):
        @pl.when(has(order[i], other))
        def _():
            ra_copy(i).start()

    def rb_copy(step, way):
        i = 2 * step + way
        tiles = pl.ds(2 * way, 2) if step != 1 else pl.ds(2 - 2 * way, 2)
        q = (q2, (q1, q3)[way], (q1, q3)[way])[step]
        dst = rb1.at[way] if step == 0 else rb2.at[way, tiles]
        return remote(part.at[2 * q + c, tiles], dst, rb_send.at[i], rb_recv.at[i], ys[way], mp)

    def ra_sum(i):
        q = order[i]

        @pl.when(has(q, c))
        def _():
            ra_copy(i).wait_recv()
            part[2 * q + c] = part[2 * q + c] + ra[q]
            if i == 0:
                rb_copy(0, 0).start()
                rb_copy(0, 1).start()
            elif i < 3:
                rb_copy(1, i - 1).start()

    def rb_second():
        for way in range(2):
            q = (q1, q3)[way]

            @pl.when(has(q, c))
            def _():
                rb_copy(0, way).wait_recv()
                t = 2 * q + c
                part[t, 2 * way:2 * way + 2] = part[t, 2 * way:2 * way + 2] + rb1[way]
                rb_copy(2, way).start()

    def right_whole():
        @pl.when(active)
        def _():
            for way in range(2):
                rb_copy(1, way).wait_recv()
                rb_copy(2, way).wait_recv()
            u = (4 * dp) % NT
            for k in range(4):
                tile = part[dp, k] + rb2[0, k] + rb2[1, k]
                one = (u + k) % NT
                two = (u + NT - k) % NT
                if k == 0:
                    tall[pl.ds(pl.multiple_of(one * T, T), T), :] = tile
                else:
                    big = jnp.maximum(one, two)
                    small = jnp.minimum(one, two)
                    tall[pl.ds(pl.multiple_of(big * T, T), T), :] = tile
                    tall[pl.ds(pl.multiple_of(small * T, T), T), :] = tile.T
            for m in range(NMP):
                t28[m] = tall[RPM * m:RPM * (m + 1)]

    def r2_go(k):
        lo, n = CHUNK[k]
        r2 = (r2a, r2b)[k]

        @pl.when(active)
        def _():
            def go(i, carry):
                to = (mp + i) % NMP
                remote(t28.at[to, pl.ds(lo, n)], r2.at[NMP - i], r2_send.at[k], r2_recv.at[k], dp, to).start()
                return carry

            lax.fori_loop(1, NMP, go, 0)
            r2[0] = t28[mp, lo:lo + n]

    def r3_copy(k, i):
        o = (dp + i) % NDP
        s3, r3 = ((s3a, r3a), (s3b, r3b))[k]
        return remote(s3.at[o], r3.at[dp], r3_send.at[k, i], r3_recv.at[k, dp], o, mp)

    def r3_go(k):
        n = CHUNK[k][1]
        s3, r3 = ((s3a, r3a), (s3b, r3b))[k]
        r2 = (r2a, r2b)[k]

        @pl.when(active)
        def _():
            everything = r2.at[pl.ds(1, NMP - 1)]
            pltpu.make_async_copy(everything, everything, r2_recv.at[k]).wait()
            for o in range(NDP):
                for s in range(CAP):
                    s3[o, n * s:n * (s + 1), :] = r2[tab[0, o * CAP + s]]
            for i in range(1, NDP):
                r3_copy(k, i).start()
            r3[dp] = s3[dp]

    def left_part(l):
        for g in range(NX):
            for i in range(NZ):
                lo = NX * T * l + 16 * NX * i + 16 * g
                a[l, g, i] = h[lo:lo + 16, :]
        g = a[l].reshape(NX * T, RB)
        block = lax.dot_general(g, g, (((1,), (1,)), ((), ())), preferred_element_type=F32)
        for v in range(4):
            for i, (r, s) in enumerate(LEFT_TILES[v]):
                lp[l, v, i] = block[r * T:(r + 1) * T, s * T:(s + 1) * T]

    def by_parity(value, fn):
        @pl.when(value % 2 == 0)
        def _():
            fn(3)

        @pl.when(value % 2 == 1)
        def _():
            fn(2)

    def lx_copy(l, step, way, n):
        i = 2 * step + way
        v = ((x + 2, x + 1, x + 1), (x + 2, x + 3, x + 3))[way][step]
        v = (v + 4 - l) % 4
        lo = half * way if step != 1 else half * (1 - way)
        tiles = pl.ds(0, n)
        part_rows = pl.ds(lo, half)
        dst = lx1.at[l, way, tiles] if step == 0 else lx2.at[l, way, tiles, part_rows]
        src = lp.at[l, v, tiles, part_rows]
        return remote(src, dst, lx_send.at[l, i], lx_recv.at[l, i], dp, xs[way])

    def lx_start(l, step):
        def go(n):
            lx_copy(l, step, 0, n).start()
            lx_copy(l, step, 1, n).start()

        by_parity(x + 4 - l + (0 if step == 0 else 1), go)

    def lx_second(l):
        def go(n):
            for way in range(2):
                lx_copy(l, 0, way, n).wait_recv()
                v = (x + (1, 3)[way] + 4 - l) % 4
                cut = slice(half * way, half * (way + 1))
                lp[l, v, :n, cut] = lp[l, v, :n, cut] + lx1[l, way, :n]
                lx_copy(l, 2, way, n).start()

        by_parity(x + 1 + 4 - l, go)

    def zz(k):
        return (z + NZ + k) % NZ

    def lz_copy(l, i):
        to, src, dst = (
            (1, lz.at[l, zz(3)], rly.at[l, 0]),
            (-1, lz.at[l, zz(-3)], rly.at[l, 1]),
            (2, lz.at[l, zz(4), pl.ds(0, 2)], rlyh.at[l, 0]),
            (-2, lz.at[l, zz(4), pl.ds(2, 2)], rlyh.at[l, 1]),
        )[i]
        return remote(src, dst, lz_send.at[l, i], lz_recv.at[l, i], dp, zz(to) * NX + x)

    hops = (0, 1, -1, 2, -2)

    def fin_start(l, j):
        for r in range(0 if j else 1, 4):
            g = (x + 4 - r) % 4
            to = zz(hops[j])
            remote(lz.at[l, to, g], fin.at[l, 4 * j + r], fin_send.at[l], fin_recv.at[l], dp, to * NX + g).start()

    def lz_first(l):
        def go(n):
            for way in range(2):
                lx_copy(l, 1, way, n).wait_recv()
                lx_copy(l, 2, way, n).wait_recv()
            v = (x + 4 - l) % 4
            tiles = [lp[l, v, i] + lx2[l, 0, i] + lx2[l, 1, i] for i in range(n)]

            def put(g, tile):
                lz[l, :, g] = tile.reshape(NZ, 16, T)

            if n == 3:
                w = v // 2
                put(w, tiles[0])
                put(w + 2, tiles[1])
                put(w + 1, tiles[2])
                put((w + 3) % 4, tiles[2].T)
            else:
                put(0, tiles[0])
                put(v, tiles[0].T)
                put(2, tiles[1])
                put((v + 2) % 4, tiles[1].T)

        by_parity(x + 4 - l, go)
        for i in (2, 3, 0, 1):
            lz_copy(l, i).start()
        for j in (1, 2, 0):
            fin_start(l, j)
        fin[l, 0] = lz[l, z, x]

    def lz_second(l):
        for way in range(2):
            t = (zz(2), zz(-2))[way]
            lz_copy(l, way).wait_recv()
            lz_copy(l, 2 + way).wait_recv()
            lz[l, t] = lz[l, t] + rly[l, way]
            lz[l, t, 2 * way:2 * way + 2] = lz[l, t, 2 * way:2 * way + 2] + rlyh[l, way]
            fin_start(l, 3 + way)

    def lz_last(l):
        everything = fin.at[l, pl.ds(1, 19)]
        pltpu.make_async_copy(everything, everything, fin_recv.at[l]).wait()
        row = []
        for g in range(4):
            r = (g + l) % 4
            row.append(fin[l, r] + fin[l, 4 + r] + fin[l, 8 + r] + fin[l, 12 + r] + fin[l, 16 + r])
        row = jnp.concatenate(row, axis=1)
        total = None
        for _ in range(3):
            piece = row.astype(BF16)
            row = row - piece.astype(F32)
            term = jnp.dot(piece, perm[...], preferred_element_type=F32)
            total = term if total is None else total + term
        left_ref[l] = total

    zh = 8 * NX

    def z_part():
        g = h[2 * NX * T:3 * NX * T, :]
        block = lax.dot_general(g, g, (((1,), (1,)), ((), ())), preferred_element_type=F32)
        zg[...] = block.reshape(NZ, 16 * NX, NX * T)

    def zr_copy(s, way):
        sign = 1 - 2 * way
        src = zg.at[zz(sign * (5 - s))]
        if s == 1:
            src, dst = zg.at[zz(4), pl.ds(way * zh, zh)], zr1.at[way]
        else:
            dst = zr2.at[way, s - 2]
        return remote(src, dst, zr_send.at[way, s - 1], zr_recv.at[way, s - 1], dp, zz(sign) * NX + x)

    def zr_start(s):
        for way in range(2):
            zr_copy(s, way).start()

    def zr_next(s):
        for way in range(2):
            sign = 1 - 2 * way
            t = zz(sign * (4 - s))
            zr_copy(s, way).wait_recv()
            if s == 1:
                cut = slice(way * zh, (way + 1) * zh)
                zg[t, cut] = zg[t, cut] + zr1[way]
            else:
                zg[t] = zg[t] + zr2[way, s - 2]
            if s < 4:
                zr_copy(s + 1, way).start()

    def x_rows(to):
        return pl.ds(pl.multiple_of(16 * to, 16), 16)

    def zx_start():
        for r in range(1, NX):
            to = (x + r) % NX
            remote(zg.at[z, x_rows(to)], zx.at[r - 1], zx_send, zx_recv, dp, z * NX + to).start()

    def zx_last():
        pltpu.make_async_copy(zx, zx, zx_recv).wait()
        left_ref[2] = zg[z, x_rows(x)] + zx[0] + zx[1] + zx[2]

    def make_perm():
        p = lax.broadcasted_iota(jnp.int32, (NX * T, NX * T), 0)
        q = lax.broadcasted_iota(jnp.int32, (NX * T, NX * T), 1)
        place = ((p // 16) % NZ) * (16 * NX) + (p // T) * 16 + p % 16
        perm[...] = (place == q).astype(F32).astype(BF16)

    def make_table():
        lane = lax.broadcasted_iota(jnp.int32, (8, T), 1)
        lane_owner = (lane * 43) >> 8
        lane_rank = lane - lane_owner * CAP
        seen = jnp.zeros((8, T), jnp.int32)
        found = jnp.zeros((8, T), jnp.int32)
        mine = jnp.int32(0)
        for b in range(NMP):
            o = owners_ref[0, b]
            same = lane_owner == o
            found = jnp.where(same & (seen == lane_rank), b, found)
            seen = seen + same.astype(jnp.int32)
            mine = mine + (o == dp).astype(jnp.int32)
        tabv[...] = (found - mp + NMP) % NMP
        cp = pltpu.make_async_copy(tabv, tab, tab_sem)
        cp.start()
        cp.wait()
        valid = [(k < mine).astype(F32) for k in range(CAP)]
        for k in range(CAP):
            scale_ref[k] = BETA * valid[k]
        return valid

    def right_out(k, valid):
        lo, n = CHUNK[k]
        r3 = (r3a, r3b)[k]
        for d in range(NT):
            @pl.when(dp != d)
            def _():
                pltpu.make_async_copy(r3.at[d], r3.at[d], r3_recv.at[k, d]).wait()

        first = (RPM * mp + lo) // T
        last = (RPM * mp + lo + n - 1) // T
        row = lax.broadcasted_iota(jnp.int32, (n, T), 0) + (RPM * mp + lo)
        upper = row < last * T
        for g in range(NT):
            one = (g + first) % NT
            two = (g + last) % NT
            for s in range(CAP):
                cut = slice(n * s, n * (s + 1))
                value = jnp.where(upper, r3[one, cut, :], r3[two, cut, :])
                right_ref[s, lo:lo + n, g * T:(g + 1) * T] = value * valid[s]

    for cp in load_h:
        cp.wait()
    for q in range(4):
        right_part(q)
    pl.semaphore_wait(barrier, NMP - 1 + NDP - 1)
    for i in range(4):
        ra_go(i)
    z_part()
    zr_start(1)
    left_part(0)
    lx_start(0, 0)
    lx_start(0, 1)
    ra_sum(0)
    ra_sum(1)
    ra_sum(2)
    left_part(1)
    lx_start(1, 0)
    lx_start(1, 1)
    ra_sum(3)
    valid = make_table()
    zr_next(1)
    lx_second(0)
    rb_second()
    lx_second(1)
    make_perm()
    zr_next(2)
    lz_first(0)
    right_whole()
    r2_go(0)
    r2_go(1)
    zr_next(3)
    lz_second(0)
    lz_first(1)
    zr_next(4)
    zx_start()
    lz_second(1)
    r3_go(0)
    lz_last(0)
    lz_last(1)
    zx_last()
    r3_go(1)
    right_out(0, valid)
    right_out(1, valid)

    for i in range(NY):
        @pl.when(has(order[i], other))
        def _():
            ra_copy(i).wait_send()

    @pl.when(has(q2, c))
    def _():
        rb_copy(0, 0).wait_send()
        rb_copy(0, 1).wait_send()

    for way in range(2):
        @pl.when(has((q1, q3)[way], c))
        def _():
            rb_copy(1, way).wait_send()
            rb_copy(2, way).wait_send()

    for l in range(2):
        for step in range(3):
            def done(n):
                lx_copy(l, step, 0, n).wait_send()
                lx_copy(l, step, 1, n).wait_send()

            by_parity(x + 4 - l + (0 if step == 0 else 1), done)
        for i in range(4):
            lz_copy(l, i).wait_send()
        sent = fin.at[l, pl.ds(1, 19)]
        pltpu.make_async_copy(sent, sent, fin_send.at[l]).wait()

    for way in range(2):
        for s in range(1, 5):
            zr_copy(s, way).wait_send()
    pltpu.make_async_copy(zx, zx, zx_send).wait()

    @pl.when(active)
    def _():
        for k in range(2):
            sent = (r2a, r2b)[k].at[pl.ds(1, NMP - 1)]
            pltpu.make_async_copy(sent, sent, r2_send.at[k]).wait()
            for i in range(1, NDP):
                r3_copy(k, i).wait_send()


def per_device(gradient, owners, left_old, right_old):
    rows = gradient.shape[0]
    dma = pltpu.SemaphoreType.DMA
    na, nb = CHUNK[0][1], CHUNK[1][1]
    left_gram, right_gram, scale = pl.pallas_call(
        kernel,
        out_shape=(
            jax.ShapeDtypeStruct((3, 16, 512), F32),
            jax.ShapeDtypeStruct((CAP, RPM, RB), F32),
            jax.ShapeDtypeStruct((CAP,), F32),
        ),
        in_specs=[
            pl.BlockSpec(memory_space=pl.ANY),
            pl.BlockSpec(memory_space=pltpu.SMEM),
        ],
        out_specs=(
            pl.BlockSpec(memory_space=pltpu.VMEM),
            pl.BlockSpec(memory_space=pltpu.VMEM),
            pl.BlockSpec(memory_space=pltpu.SMEM),
        ),
        scratch_shapes=[
            pltpu.VMEM((rows, RB), BF16),
            pltpu.VMEM((2, NX, NZ, 16, RB), BF16),
            pltpu.VMEM((NDP, 4, T, T), F32),
            pltpu.VMEM((NY, 4, T, T), F32),
            pltpu.VMEM((2, 2, T, T), F32),
            pltpu.VMEM((2, 4, T, T), F32),
            pltpu.VMEM((RB, T), F32),
            pltpu.VMEM((NMP, RPM, T), F32),
            pltpu.VMEM((NMP, na, T), F32),
            pltpu.VMEM((NMP, nb, T), F32),
            pltpu.VMEM((NDP, CAP * na, T), F32),
            pltpu.VMEM((NDP, CAP * nb, T), F32),
            pltpu.VMEM((NDP, CAP * na, T), F32),
            pltpu.VMEM((NDP, CAP * nb, T), F32),
            pltpu.VMEM((2, 4, 3, T, T), F32),
            pltpu.VMEM((2, 2, 3, T // 2, T), F32),
            pltpu.VMEM((2, 2, 3, T, T), F32),
            pltpu.VMEM((2, NZ, 4, 16, T), F32),
            pltpu.VMEM((2, 2, 4, 16, T), F32),
            pltpu.VMEM((2, 2, 2, 16, T), F32),
            pltpu.VMEM((2, 20, 16, T), F32),
            pltpu.VMEM((NZ, 16 * NX, NX * T), F32),
            pltpu.VMEM((2, 8 * NX, NX * T), F32),
            pltpu.VMEM((2, 3, 16 * NX, NX * T), F32),
            pltpu.VMEM((3, 16, NX * T), F32),
            pltpu.VMEM((4 * T, 4 * T), BF16),
            pltpu.VMEM((8, T), jnp.int32),
            pltpu.SMEM((8, T), jnp.int32),
            dma((4,)), dma,
            dma((NY,)), dma((NY,)), dma((6,)), dma((6,)),
            dma((2,)), dma((2,)), dma((2, NDP)), dma((2, NDP)),
            dma((2, 6)), dma((2, 6)), dma((2, 4)), dma((2, 4)), dma((2,)), dma((2,)),
            dma((2, 4)), dma((2, 4)), dma, dma,
        ],
        compiler_params=pltpu.CompilerParams(
            collective_id=0, has_side_effects=True, vmem_limit_bytes=105 * 512 * 1024
        ),
        name="stats",
    )(gradient, owners.reshape(1, NMP))
    left_stats = BETA * left_old + left_gram
    right_stats = scale[:, None, None] * right_old + right_gram
    return left_stats, right_stats


def solution(mesh):
    in_specs = (P("dp", "mp"), P(), P("dp", "mp", None), P("dp", "mp", None))
    out_specs = (P("dp", "mp", None), P("dp", "mp", None))
    return jax.shard_map(
        per_device, mesh=mesh, in_specs=in_specs, out_specs=out_specs, check_vma=False
    )
```

```python
import jax
import jax.numpy as jnp
from jax import lax
from jax.experimental import pallas as pl
from jax.experimental.pallas import tpu as pltpu
from jax.sharding import PartitionSpec as P

BETA = 0.95
F32 = jnp.float32
BF16 = jnp.bfloat16
RB = 896
T = 128
NT = 7
NMP = 32
NDP = 8
CAP = 6
RPM = 28
NY = 4
NX = 4
NZ = 8

CHUNK = ((0, 16), (16, 12))

LEFT_TILES = (
    ((0, 0), (2, 2), (1, 3)),
    ((0, 1), (2, 3)),
    ((1, 1), (3, 3), (2, 0)),
    ((0, 3), (2, 1)),
)


def remote(src, dst, send_sem, recv_sem, dp, mp):
    return pltpu.make_async_remote_copy(
        src_ref=src,
        dst_ref=dst,
        send_sem=send_sem,
        recv_sem=recv_sem,
        device_id=(dp, mp),
        device_id_type=pl.DeviceIdType.MESH,
    )


def kernel(
    grad_ref, owners_ref, left_ref, right_ref,
    h, a, part, ra, rb1, rb2, tall, t28, r2a, r2b, s3a, s3b, r3a, r3b,
    lp, lx1, lx2, lz, rly, rlyh, fin, zg, zr, zx, perm, own, tabv, tab,
    in_sem, tab_sem, ra_send, ra_recv, rb_send, rb_recv,
    r2_send, r2_recv, r3_send, r3_recv,
    lx_send, lx_recv, lz_send, lz_recv, fin_send, fin_recv,
    zr_send, zr_recv, zx_send, zx_recv,
):
    dp = lax.axis_index("dp")
    mp = lax.axis_index("mp")
    y, c = dp // 2, dp % 2
    z, x = mp // NX, mp % NX
    other = 1 - c
    half = T // 2
    xs = (z * NX + (x + 1) % NX, z * NX + (x + 3) % NX)
    ys = (2 * ((y + 1) % NY) + c, 2 * ((y + 3) % NY) + c)
    active = dp < NT

    def has(q, core):
        return 2 * q + core < NT

    nb = NX * T
    load_h = {}
    for l in (2, 0, 1):
        load_h[l] = pltpu.make_async_copy(grad_ref.at[pl.ds(l * nb, nb)], h.at[pl.ds(l * nb, nb)], in_sem.at[l])
        load_h[l].start()
    load_owners = pltpu.make_async_copy(owners_ref, own, in_sem.at[3])
    load_owners.start()

    barrier = pltpu.get_barrier_semaphore()

    def hello_mp(i, carry):
        pl.semaphore_signal(barrier, inc=1, device_id=(dp, (mp + i) % NMP), device_id_type=pl.DeviceIdType.MESH)
        return carry

    def hello_dp(i, carry):
        pl.semaphore_signal(barrier, inc=1, device_id=((dp + i) % NDP, mp), device_id_type=pl.DeviceIdType.MESH)
        return carry

    lax.fori_loop(1, NDP, hello_dp, 0)
    lax.fori_loop(1, NMP, hello_mp, 0)

    def right_part(l, q):
        lo = 2 * T * q
        wide = min(2 * T, RB - lo)
        some = slice(l * nb, (l + 1) * nb)
        block = lax.dot_general(
            h[some, lo:RB], h[some, lo:lo + wide], (((0,), (0,)), ((), ())), preferred_element_type=F32
        )
        for col in range(2 * q, 2 * q + wide // T):
            for row in range(col, NT):
                d = (row + col) % NT
                u = (4 * d) % NT
                k = min((row - u) % NT, (u - row) % NT)
                i, j = (row - 2 * q) * T, (col - 2 * q) * T
                tile = block[i:i + T, j:j + T]
                part[d, k] = tile if l == 2 else part[d, k] + tile

    order = [(y + k) % NY for k in (2, 1, 3, 0)]
    q2, q1, q3, q0 = order

    def ra_copy(i):
        q = order[i]
        return remote(part.at[2 * q + other], ra.at[q], ra_send.at[i], ra_recv.at[i], dp + 1 - 2 * c, mp)

    def ra_go(i):
        @pl.when(has(order[i], other))
        def _():
            ra_copy(i).start()

    def rb_copy(step, way):
        i = 2 * step + way
        tiles = pl.ds(2 * way, 2) if step != 1 else pl.ds(2 - 2 * way, 2)
        q = (q2, (q1, q3)[way], (q1, q3)[way])[step]
        dst = rb1.at[way] if step == 0 else rb2.at[way, tiles]
        return remote(part.at[2 * q + c, tiles], dst, rb_send.at[i], rb_recv.at[i], ys[way], mp)

    def ra_sum(i):
        q = order[i]

        @pl.when(has(q, c))
        def _():
            ra_copy(i).wait_recv()
            part[2 * q + c] = part[2 * q + c] + ra[q]
            if i == 0:
                rb_copy(0, 0).start()
                rb_copy(0, 1).start()
            elif i < 3:
                rb_copy(1, i - 1).start()

    def rb_second():
        for way in range(2):
            q = (q1, q3)[way]

            @pl.when(has(q, c))
            def _():
                rb_copy(0, way).wait_recv()
                t = 2 * q + c
                part[t, 2 * way:2 * way + 2] = part[t, 2 * way:2 * way + 2] + rb1[way]
                rb_copy(2, way).start()

    def right_whole():
        @pl.when(active)
        def _():
            for way in range(2):
                rb_copy(1, way).wait_recv()
                rb_copy(2, way).wait_recv()
            u = (4 * dp) % NT
            for k in range(4):
                tile = part[dp, k] + rb2[0, k] + rb2[1, k]
                one = (u + k) % NT
                two = (u + NT - k) % NT
                if k == 0:
                    tall[pl.ds(pl.multiple_of(one * T, T), T), :] = tile
                else:
                    big = jnp.maximum(one, two)
                    small = jnp.minimum(one, two)
                    tall[pl.ds(pl.multiple_of(big * T, T), T), :] = tile
                    tall[pl.ds(pl.multiple_of(small * T, T), T), :] = tile.T
            for m in range(NMP):
                t28[m] = tall[RPM * m:RPM * (m + 1)]

    def r2_go(k):
        lo, n = CHUNK[k]
        r2 = (r2a, r2b)[k]

        @pl.when(active)
        def _():
            for i in range(1, NMP):
                to = (mp + i) % NMP
                remote(t28.at[to, pl.ds(lo, n)], r2.at[NMP - i], r2_send.at[k], r2_recv.at[k], dp, to).start()
            r2[0] = t28[mp, lo:lo + n]

    def r3_copy(k, i):
        o = (dp + i) % NDP
        s3, r3 = ((s3a, r3a), (s3b, r3b))[k]
        return remote(s3.at[o], r3.at[dp], r3_send.at[k, i], r3_recv.at[k, dp], o, mp)

    def r3_go(k):
        n = CHUNK[k][1]
        s3, r3 = ((s3a, r3a), (s3b, r3b))[k]
        r2 = (r2a, r2b)[k]

        @pl.when(active)
        def _():
            everything = r2.at[pl.ds(1, NMP - 1)]
            pltpu.make_async_copy(everything, everything, r2_recv.at[k]).wait()
            for o in range(NDP):
                for s in range(CAP):
                    s3[o, n * s:n * (s + 1), :] = r2[tab[0, o * CAP + s]]
            for i in range(1, NDP):
                r3_copy(k, i).start()
            r3[dp] = s3[dp]

    def left_part(l):
        for g in range(NX):
            for i in range(NZ):
                lo = NX * T * l + 16 * NX * i + 16 * g
                a[l, g, i] = h[lo:lo + 16, :]
        g = a[l].reshape(NX * T, RB)
        block = lax.dot_general(g, g, (((1,), (1,)), ((), ())), preferred_element_type=F32)
        for v in range(4):
            for i, (r, s) in enumerate(LEFT_TILES[v]):
                lp[l, v, i] = block[r * T:(r + 1) * T, s * T:(s + 1) * T]

    def by_parity(value, fn):
        @pl.when(value % 2 == 0)
        def _():
            fn(3)

        @pl.when(value % 2 == 1)
        def _():
            fn(2)

    def lx_copy(l, step, way, n):
        i = 2 * step + way
        v = ((x + 2, x + 1, x + 1), (x + 2, x + 3, x + 3))[way][step]
        v = (v + 4 - l) % 4
        lo = half * way if step != 1 else half * (1 - way)
        tiles = pl.ds(0, n)
        part_rows = pl.ds(lo, half)
        dst = lx1.at[l, way, tiles] if step == 0 else lx2.at[l, way, tiles, part_rows]
        src = lp.at[l, v, tiles, part_rows]
        return remote(src, dst, lx_send.at[l, i], lx_recv.at[l, i], dp, xs[way])

    def lx_start(l, step):
        def go(n):
            lx_copy(l, step, 0, n).start()
            lx_copy(l, step, 1, n).start()

        by_parity(x + 4 - l + (0 if step == 0 else 1), go)

    def lx_second(l):
        def go(n):
            for way in range(2):
                lx_copy(l, 0, way, n).wait_recv()
                v = (x + (1, 3)[way] + 4 - l) % 4
                cut = slice(half * way, half * (way + 1))
                lp[l, v, :n, cut] = lp[l, v, :n, cut] + lx1[l, way, :n]
                lx_copy(l, 2, way, n).start()

        by_parity(x + 1 + 4 - l, go)

    def zz(k):
        return (z + NZ + k) % NZ

    def lz_copy(l, i):
        to, src, dst = (
            (1, lz.at[l, zz(3)], rly.at[l, 0]),
            (-1, lz.at[l, zz(-3)], rly.at[l, 1]),
            (2, lz.at[l, zz(4), pl.ds(0, 2)], rlyh.at[l, 0]),
            (-2, lz.at[l, zz(4), pl.ds(2, 2)], rlyh.at[l, 1]),
        )[i]
        return remote(src, dst, lz_send.at[l, i], lz_recv.at[l, i], dp, zz(to) * NX + x)

    hops = (0, 1, -1, 2, -2)

    def fin_start(l, j):
        for r in range(0 if j else 1, 4):
            g = (x + 4 - r) % 4
            to = zz(hops[j])
            remote(lz.at[l, to, g], fin.at[l, 4 * j + r], fin_send.at[l], fin_recv.at[l], dp, to * NX + g).start()

    def lz_first(l):
        def go(n):
            for way in range(2):
                lx_copy(l, 1, way, n).wait_recv()
                lx_copy(l, 2, way, n).wait_recv()
            v = (x + 4 - l) % 4
            tiles = [lp[l, v, i] + lx2[l, 0, i] + lx2[l, 1, i] for i in range(n)]

            def put(g, tile):
                lz[l, :, g] = tile.reshape(NZ, 16, T)

            if n == 3:
                w = v // 2
                put(w, tiles[0])
                put(w + 2, tiles[1])
                put(w + 1, tiles[2])
                put((w + 3) % 4, tiles[2].T)
            else:
                put(0, tiles[0])
                put(v, tiles[0].T)
                put(2, tiles[1])
                put((v + 2) % 4, tiles[1].T)

        by_parity(x + 4 - l, go)
        for i in (2, 3, 0, 1):
            lz_copy(l, i).start()
        for j in (1, 2, 0):
            fin_start(l, j)
        fin[l, 0] = lz[l, z, x]

    def lz_second(l):
        for way in range(2):
            t = (zz(2), zz(-2))[way]
            lz_copy(l, way).wait_recv()
            lz_copy(l, 2 + way).wait_recv()
            lz[l, t] = lz[l, t] + rly[l, way]
            lz[l, t, 2 * way:2 * way + 2] = lz[l, t, 2 * way:2 * way + 2] + rlyh[l, way]
            fin_start(l, 3 + way)

    def lz_last(l):
        everything = fin.at[l, pl.ds(1, 19)]
        pltpu.make_async_copy(everything, everything, fin_recv.at[l]).wait()
        row = []
        for g in range(4):
            r = (g + l) % 4
            row.append(fin[l, r] + fin[l, 4 + r] + fin[l, 8 + r] + fin[l, 12 + r] + fin[l, 16 + r])
        row = jnp.concatenate(row, axis=1)
        total = None
        for _ in range(3):
            piece = row.astype(BF16)
            row = row - piece.astype(F32)
            term = jnp.dot(piece, perm[...], preferred_element_type=F32)
            total = term if total is None else total + term
        left_ref[l] = total

    zh = 8 * NX

    def z_part():
        g = h[2 * NX * T:3 * NX * T, :]
        block = lax.dot_general(g, g, (((1,), (1,)), ((), ())), preferred_element_type=F32)
        zg[...] = block.reshape(NZ, 16 * NX, NX * T)

    def zr_copy(s, way, late):
        sign = 1 - 2 * way
        cut = pl.ds((1 - way if late else way) * zh, zh)
        i = s + 2 if late else s - 1
        src = zg.at[zz(sign * (5 - s)), cut]
        return remote(src, zr.at[way, i], zr_send.at[way, i], zr_recv.at[way, i], dp, zz(sign) * NX + x)

    def zr_start(s, late):
        for way in range(2):
            zr_copy(s, way, late).start()

    def zr_next(s, late):
        for way in range(2):
            sign = 1 - 2 * way
            t = zz(sign * (4 - s))
            lo = (1 - way if late else way) * zh
            zr_copy(s, way, late).wait_recv()
            zg[t, lo:lo + zh] = zg[t, lo:lo + zh] + zr[way, s + 2 if late else s - 1]
            if s < 4:
                zr_copy(s + 1, way, late).start()

    def x_rows(to):
        return pl.ds(pl.multiple_of(16 * to, 16), 16)

    def zx_start():
        for r in range(1, NX):
            to = (x + r) % NX
            remote(zg.at[z, x_rows(to)], zx.at[r - 1], zx_send, zx_recv, dp, z * NX + to).start()

    def zx_last():
        pltpu.make_async_copy(zx, zx, zx_recv).wait()
        left_ref[2] = zg[z, x_rows(x)] + zx[0] + zx[1] + zx[2]

    def make_perm():
        p = lax.broadcasted_iota(jnp.int32, (NX * T, NX * T), 0)
        q = lax.broadcasted_iota(jnp.int32, (NX * T, NX * T), 1)
        place = ((p // 16) % NZ) * (16 * NX) + (p // T) * 16 + p % 16
        perm[...] = (place == q).astype(F32).astype(BF16)

    def make_table():
        load_owners.wait()
        lane = lax.broadcasted_iota(jnp.int32, (8, T), 1)
        lane_owner = (lane * 43) >> 8
        lane_rank = lane - lane_owner * CAP
        seen = jnp.zeros((8, T), jnp.int32)
        found = jnp.zeros((8, T), jnp.int32)
        mine = jnp.int32(0)
        for b in range(NMP):
            o = own[0, b]
            same = lane_owner == o
            found = jnp.where(same & (seen == lane_rank), b, found)
            seen = seen + same.astype(jnp.int32)
            mine = mine + (o == dp).astype(jnp.int32)
        tabv[...] = (found - mp + NMP) % NMP
        cp = pltpu.make_async_copy(tabv, tab, tab_sem)
        cp.start()
        cp.wait()
        return [jnp.where(k < mine, F32(0), F32(jnp.nan)) for k in range(CAP)]

    def right_out(k, empty):
        lo, n = CHUNK[k]
        r3 = (r3a, r3b)[k]
        for d in range(NT):
            @pl.when(dp != d)
            def _():
                pltpu.make_async_copy(r3.at[d], r3.at[d], r3_recv.at[k, d]).wait()

        first = (RPM * mp + lo) // T
        last = (RPM * mp + lo + n - 1) // T
        row = lax.broadcasted_iota(jnp.int32, (n, T), 0) + (RPM * mp + lo)
        upper = row < last * T
        for g in range(NT):
            one = (g + first) % NT
            two = (g + last) % NT
            for s in range(CAP):
                cut = slice(n * s, n * (s + 1))
                value = jnp.where(upper, r3[one, cut, :], r3[two, cut, :])
                right_ref[s, lo:lo + n, g * T:(g + 1) * T] = value + empty[s]

    for l in (2, 0, 1):
        load_h[l].wait()
        for q in range(4):
            right_part(l, q)
    pl.semaphore_wait(barrier, NMP - 1 + NDP - 1)
    for i in range(4):
        ra_go(i)
    z_part()
    zr_start(1, False)
    zr_start(2, True)
    left_part(0)
    lx_start(0, 0)
    lx_start(0, 1)
    ra_sum(0)
    ra_sum(1)
    ra_sum(2)
    left_part(1)
    zr_next(1, False)
    lx_second(0)
    lx_start(1, 0)
    lx_start(1, 1)
    zr_next(2, True)
    ra_sum(3)
    empty = make_table()
    rb_second()
    zr_next(2, False)
    zr_next(3, True)
    lz_first(0)
    zr_next(3, False)
    lx_second(1)
    zr_next(4, True)
    right_whole()
    r2_go(0)
    lz_second(0)
    zr_next(4, False)
    zx_start()
    r2_go(1)
    lz_first(1)
    make_perm()
    lz_last(0)
    r3_go(0)
    zx_last()
    r3_go(1)
    lz_second(1)
    right_out(0, empty)
    lz_last(1)
    right_out(1, empty)

    for i in range(NY):
        @pl.when(has(order[i], other))
        def _():
            ra_copy(i).wait_send()

    @pl.when(has(q2, c))
    def _():
        rb_copy(0, 0).wait_send()
        rb_copy(0, 1).wait_send()

    for way in range(2):
        @pl.when(has((q1, q3)[way], c))
        def _():
            rb_copy(1, way).wait_send()
            rb_copy(2, way).wait_send()

    for l in range(2):
        for step in range(3):
            def done(n):
                lx_copy(l, step, 0, n).wait_send()
                lx_copy(l, step, 1, n).wait_send()

            by_parity(x + 4 - l + (0 if step == 0 else 1), done)
        for i in range(4):
            lz_copy(l, i).wait_send()
        sent = fin.at[l, pl.ds(1, 19)]
        pltpu.make_async_copy(sent, sent, fin_send.at[l]).wait()

    for way in range(2):
        for s in range(1, 5):
            zr_copy(s, way, False).wait_send()
            if s > 1:
                zr_copy(s, way, True).wait_send()
    pltpu.make_async_copy(zx, zx, zx_send).wait()

    @pl.when(active)
    def _():
        for k in range(2):
            sent = (r2a, r2b)[k].at[pl.ds(1, NMP - 1)]
            pltpu.make_async_copy(sent, sent, r2_send.at[k]).wait()
            for i in range(1, NDP):
                r3_copy(k, i).wait_send()


def per_device(gradient, owners, left_old, right_old):
    rows = gradient.shape[0]
    dma = pltpu.SemaphoreType.DMA
    na, nb = CHUNK[0][1], CHUNK[1][1]
    left_gram, right_gram = pl.pallas_call(
        kernel,
        out_shape=(
            jax.ShapeDtypeStruct((3, 16, 512), F32),
            jax.ShapeDtypeStruct((CAP, RPM, RB), F32),
        ),
        in_specs=[
            pl.BlockSpec(memory_space=pl.ANY),
            pl.BlockSpec(memory_space=pl.ANY),
        ],
        out_specs=(
            pl.BlockSpec(memory_space=pltpu.VMEM),
            pl.BlockSpec(memory_space=pltpu.VMEM),
        ),
        scratch_shapes=[
            pltpu.VMEM((rows, RB), BF16),
            pltpu.VMEM((2, NX, NZ, 16, RB), BF16),
            pltpu.VMEM((NDP, 4, T, T), F32),
            pltpu.VMEM((NY, 4, T, T), F32),
            pltpu.VMEM((2, 2, T, T), F32),
            pltpu.VMEM((2, 4, T, T), F32),
            pltpu.VMEM((RB, T), F32),
            pltpu.VMEM((NMP, RPM, T), F32),
            pltpu.VMEM((NMP, na, T), F32),
            pltpu.VMEM((NMP, nb, T), F32),
            pltpu.VMEM((NDP, CAP * na, T), F32),
            pltpu.VMEM((NDP, CAP * nb, T), F32),
            pltpu.VMEM((NDP, CAP * na, T), F32),
            pltpu.VMEM((NDP, CAP * nb, T), F32),
            pltpu.VMEM((2, 4, 3, T, T), F32),
            pltpu.VMEM((2, 2, 3, T // 2, T), F32),
            pltpu.VMEM((2, 2, 3, T, T), F32),
            pltpu.VMEM((2, NZ, 4, 16, T), F32),
            pltpu.VMEM((2, 2, 4, 16, T), F32),
            pltpu.VMEM((2, 2, 2, 16, T), F32),
            pltpu.VMEM((2, 20, 16, T), F32),
            pltpu.VMEM((NZ, 16 * NX, NX * T), F32),
            pltpu.VMEM((2, 7, 8 * NX, NX * T), F32),
            pltpu.VMEM((3, 16, NX * T), F32),
            pltpu.VMEM((4 * T, 4 * T), BF16),
            pltpu.SMEM((1, NMP), jnp.int32),
            pltpu.VMEM((8, T), jnp.int32),
            pltpu.SMEM((8, T), jnp.int32),
            dma((4,)), dma,
            dma((NY,)), dma((NY,)), dma((6,)), dma((6,)),
            dma((2,)), dma((2,)), dma((2, NDP)), dma((2, NDP)),
            dma((2, 6)), dma((2, 6)), dma((2, 4)), dma((2, 4)), dma((2,)), dma((2,)),
            dma((2, 7)), dma((2, 7)), dma, dma,
        ],
        compiler_params=pltpu.CompilerParams(
            collective_id=0, has_side_effects=True, vmem_limit_bytes=105 * 512 * 1024
        ),
        name="stats",
    )(gradient, owners.reshape(1, NMP))
    left_stats = BETA * left_old + left_gram
    right_stats = jnp.where(jnp.isnan(right_gram), 0.0, BETA * right_old + right_gram)
    return left_stats, right_stats


def solution(mesh):
    in_specs = (P("dp", "mp"), P(), P("dp", "mp", None), P("dp", "mp", None))
    out_specs = (P("dp", "mp", None), P("dp", "mp", None))
    return jax.shard_map(
        per_device, mesh=mesh, in_specs=in_specs, out_specs=out_specs, check_vma=False
    )
```

```python
import jax
import jax.numpy as jnp
from jax import lax
from jax.experimental import pallas as pl
from jax.experimental.pallas import tpu as pltpu
from jax.sharding import PartitionSpec as P

BETA = 0.95
F32 = jnp.float32
BF16 = jnp.bfloat16
RB = 896
T = 128
NT = 7
NMP = 32
NDP = 8
CAP = 6
RPM = 28
NY = 4
NX = 4
NZ = 8

CHUNK = ((0, 16), (16, 12))

LEFT_TILES = (
    ((0, 0), (2, 2), (1, 3)),
    ((0, 1), (2, 3)),
    ((1, 1), (3, 3), (2, 0)),
    ((0, 3), (2, 1)),
)


def remote(src, dst, send_sem, recv_sem, dp, mp):
    return pltpu.make_async_remote_copy(
        src_ref=src,
        dst_ref=dst,
        send_sem=send_sem,
        recv_sem=recv_sem,
        device_id=(dp, mp),
        device_id_type=pl.DeviceIdType.MESH,
    )


def kernel(
    grad_ref, owners_ref, left_ref, right_ref,
    h, a, part, ra, rb1, rb2, tall, t28, r2a, r2b, s3a, s3b, r3a, r3b,
    lp, lx1, lx2, lz, rly, rlyh, fin, zg, zr, zx, perm, own, tabv, tab,
    in_sem, tab_sem, ra_send, ra_recv, rb_send, rb_recv,
    r2_send, r2_recv, r3_send, r3_recv,
    lx_send, lx_recv, lz_send, lz_recv, fin_send, fin_recv,
    zr_send, zr_recv, zx_send, zx_recv,
):
    dp = lax.axis_index("dp")
    mp = lax.axis_index("mp")
    y, c = dp // 2, dp % 2
    z, x = mp // NX, mp % NX
    other = 1 - c
    half = T // 2
    xs = (z * NX + (x + 1) % NX, z * NX + (x + 3) % NX)
    ys = (2 * ((y + 1) % NY) + c, 2 * ((y + 3) % NY) + c)
    active = dp < NT

    def has(q, core):
        return 2 * q + core < NT

    nb = NX * T
    load_h = {}
    for l in (2, 0, 1):
        load_h[l] = pltpu.make_async_copy(grad_ref.at[pl.ds(l * nb, nb)], h.at[pl.ds(l * nb, nb)], in_sem.at[l])
        load_h[l].start()
    load_owners = pltpu.make_async_copy(owners_ref, own, in_sem.at[3])
    load_owners.start()

    barrier = pltpu.get_barrier_semaphore()

    def hello_mp(i, carry):
        pl.semaphore_signal(barrier, inc=1, device_id=(dp, (mp + i) % NMP), device_id_type=pl.DeviceIdType.MESH)
        return carry

    def hello_dp(i, carry):
        pl.semaphore_signal(barrier, inc=1, device_id=((dp + i) % NDP, mp), device_id_type=pl.DeviceIdType.MESH)
        return carry

    lax.fori_loop(1, NDP, hello_dp, 0)
    lax.fori_loop(1, NMP, hello_mp, 0)

    def right_part(l, q):
        lo = 2 * T * q
        wide = min(2 * T, RB - lo)
        some = slice(l * nb, (l + 1) * nb)
        block = lax.dot_general(
            h[some, lo:RB], h[some, lo:lo + wide], (((0,), (0,)), ((), ())), preferred_element_type=F32
        )
        for col in range(2 * q, 2 * q + wide // T):
            for row in range(col, NT):
                d = (row + col) % NT
                u = (4 * d) % NT
                k = min((row - u) % NT, (u - row) % NT)
                i, j = (row - 2 * q) * T, (col - 2 * q) * T
                tile = block[i:i + T, j:j + T]
                part[d, k] = tile if l == 2 else part[d, k] + tile

    order = [(y + k) % NY for k in (2, 1, 3, 0)]
    q2, q1, q3, q0 = order

    def ra_copy(i):
        q = order[i]
        return remote(part.at[2 * q + other], ra.at[q], ra_send.at[i], ra_recv.at[i], dp + 1 - 2 * c, mp)

    def ra_go(i):
        @pl.when(has(order[i], other))
        def _():
            ra_copy(i).start()

    def rb_copy(step, way):
        i = 2 * step + way
        tiles = pl.ds(2 * way, 2) if step != 1 else pl.ds(2 - 2 * way, 2)
        q = (q2, (q1, q3)[way], (q1, q3)[way])[step]
        dst = rb1.at[way] if step == 0 else rb2.at[way, tiles]
        return remote(part.at[2 * q + c, tiles], dst, rb_send.at[i], rb_recv.at[i], ys[way], mp)

    def ra_sum(i):
        q = order[i]

        @pl.when(has(q, c))
        def _():
            ra_copy(i).wait_recv()
            part[2 * q + c] = part[2 * q + c] + ra[q]
            if i == 0:
                rb_copy(0, 0).start()
                rb_copy(0, 1).start()
            elif i < 3:
                rb_copy(1, i - 1).start()

    def rb_second():
        for way in range(2):
            q = (q1, q3)[way]

            @pl.when(has(q, c))
            def _():
                rb_copy(0, way).wait_recv()
                t = 2 * q + c
                part[t, 2 * way:2 * way + 2] = part[t, 2 * way:2 * way + 2] + rb1[way]
                rb_copy(2, way).start()

    def right_whole():
        @pl.when(active)
        def _():
            for way in range(2):
                rb_copy(1, way).wait_recv()
                rb_copy(2, way).wait_recv()
            u = (4 * dp) % NT
            for k in range(4):
                tile = part[dp, k] + rb2[0, k] + rb2[1, k]
                one = (u + k) % NT
                two = (u + NT - k) % NT
                if k == 0:
                    tall[pl.ds(pl.multiple_of(one * T, T), T), :] = tile
                else:
                    big = jnp.maximum(one, two)
                    small = jnp.minimum(one, two)
                    tall[pl.ds(pl.multiple_of(big * T, T), T), :] = tile
                    tall[pl.ds(pl.multiple_of(small * T, T), T), :] = tile.T
            for m in range(NMP):
                t28[m] = tall[RPM * m:RPM * (m + 1)]

    def r2_go(k):
        lo, n = CHUNK[k]
        r2 = (r2a, r2b)[k]

        @pl.when(active)
        def _():
            for i in range(1, NMP):
                to = (mp + i) % NMP
                remote(t28.at[to, pl.ds(lo, n)], r2.at[NMP - i], r2_send.at[k], r2_recv.at[k], dp, to).start()
            r2[0] = t28[mp, lo:lo + n]

    def r3_copy(k, i):
        o = (dp + i) % NDP
        s3, r3 = ((s3a, r3a), (s3b, r3b))[k]
        return remote(s3.at[o], r3.at[dp], r3_send.at[k, i], r3_recv.at[k, dp], o, mp)

    def r3_go(k):
        n = CHUNK[k][1]
        s3, r3 = ((s3a, r3a), (s3b, r3b))[k]
        r2 = (r2a, r2b)[k]

        @pl.when(active)
        def _():
            everything = r2.at[pl.ds(1, NMP - 1)]
            pltpu.make_async_copy(everything, everything, r2_recv.at[k]).wait()
            for o in range(NDP):
                for s in range(CAP):
                    s3[o, n * s:n * (s + 1), :] = r2[tab[0, o * CAP + s]]
            for i in range(1, NDP):
                r3_copy(k, i).start()
            r3[dp] = s3[dp]

    def left_part(l):
        for g in range(NX):
            for i in range(NZ):
                lo = NX * T * l + 16 * NX * i + 16 * g
                a[l, g, i] = h[lo:lo + 16, :]
        g = a[l].reshape(NX * T, RB)
        block = lax.dot_general(g, g, (((1,), (1,)), ((), ())), preferred_element_type=F32)
        for v in range(4):
            for i, (r, s) in enumerate(LEFT_TILES[v]):
                lp[l, v, i] = block[r * T:(r + 1) * T, s * T:(s + 1) * T]

    def by_parity(value, fn):
        @pl.when(value % 2 == 0)
        def _():
            fn(3)

        @pl.when(value % 2 == 1)
        def _():
            fn(2)

    def lx_copy(l, step, way, n):
        i = 2 * step + way
        v = ((x + 2, x + 1, x + 1), (x + 2, x + 3, x + 3))[way][step]
        v = (v + 4 - l) % 4
        lo = half * way if step != 1 else half * (1 - way)
        tiles = pl.ds(0, n)
        part_rows = pl.ds(lo, half)
        dst = lx1.at[l, way, tiles] if step == 0 else lx2.at[l, way, tiles, part_rows]
        src = lp.at[l, v, tiles, part_rows]
        return remote(src, dst, lx_send.at[l, i], lx_recv.at[l, i], dp, xs[way])

    def lx_start(l, step):
        def go(n):
            lx_copy(l, step, 0, n).start()
            lx_copy(l, step, 1, n).start()

        by_parity(x + 4 - l + (0 if step == 0 else 1), go)

    def lx_second(l):
        def go(n):
            for way in range(2):
                lx_copy(l, 0, way, n).wait_recv()
                v = (x + (1, 3)[way] + 4 - l) % 4
                cut = slice(half * way, half * (way + 1))
                lp[l, v, :n, cut] = lp[l, v, :n, cut] + lx1[l, way, :n]
                lx_copy(l, 2, way, n).start()

        by_parity(x + 1 + 4 - l, go)

    def zz(k):
        return (z + NZ + k) % NZ

    def lz_copy(i):
        to, src, dst = (
            (1, lz.at[zz(3)], rly.at[0]),
            (-1, lz.at[zz(-3)], rly.at[1]),
            (2, lz.at[zz(4), pl.ds(0, 2)], rlyh.at[0]),
            (-2, lz.at[zz(4), pl.ds(2, 2)], rlyh.at[1]),
        )[i]
        return remote(src, dst, lz_send.at[i], lz_recv.at[i], dp, zz(to) * NX + x)

    hops = (0, 1, -1, 2, -2)

    def fin_start(j):
        for r in range(0 if j else 1, 4):
            g = (x + 4 - r) % 4
            to = zz(hops[j])
            remote(lz.at[to, g], fin.at[4 * j + r], fin_send, fin_recv, dp, to * NX + g).start()

    def lz_put(l):
        def go(n):
            for way in range(2):
                lx_copy(l, 1, way, n).wait_recv()
                lx_copy(l, 2, way, n).wait_recv()
            v = (x + 4 - l) % 4
            tiles = [lp[l, v, i] + lx2[l, 0, i] + lx2[l, 1, i] for i in range(n)]

            def put(g, tile):
                lz[:, g, l] = tile.reshape(NZ, 16, T)

            if n == 3:
                w = v // 2
                put(w, tiles[0])
                put(w + 2, tiles[1])
                put(w + 1, tiles[2])
                put((w + 3) % 4, tiles[2].T)
            else:
                put(0, tiles[0])
                put(v, tiles[0].T)
                put(2, tiles[1])
                put((v + 2) % 4, tiles[1].T)

        by_parity(x + 4 - l, go)

    def lz_first():
        for i in (2, 3, 0, 1):
            lz_copy(i).start()
        for j in (1, 2, 0):
            fin_start(j)
        fin[0] = lz[z, x]

    def lz_second():
        for way in range(2):
            t = (zz(2), zz(-2))[way]
            lz_copy(way).wait_recv()
            lz_copy(2 + way).wait_recv()
            lz[t] = lz[t] + rly[way]
            lz[t, 2 * way:2 * way + 2] = lz[t, 2 * way:2 * way + 2] + rlyh[way]
            fin_start(3 + way)

    def lz_last():
        everything = fin.at[pl.ds(1, 19)]
        pltpu.make_async_copy(everything, everything, fin_recv).wait()
        rows = []
        for l in range(2):
            row = []
            for g in range(4):
                r = (g + l) % 4
                row.append(fin[r, l] + fin[4 + r, l] + fin[8 + r, l] + fin[12 + r, l] + fin[16 + r, l])
            rows.append(jnp.concatenate(row, axis=1))
        rows = jnp.concatenate(rows, axis=0)
        total = None
        for _ in range(3):
            piece = rows.astype(BF16)
            rows = rows - piece.astype(F32)
            term = jnp.dot(piece, perm[...], preferred_element_type=F32)
            total = term if total is None else total + term
        left_ref[0] = total[:16]
        left_ref[1] = total[16:]

    zh = 8 * NX

    def z_part():
        g = h[2 * NX * T:3 * NX * T, :]
        block = lax.dot_general(g, g, (((1,), (1,)), ((), ())), preferred_element_type=F32)
        zg[...] = block.reshape(NZ, 16 * NX, NX * T)

    def zr_copy(s, way, late):
        sign = 1 - 2 * way
        cut = pl.ds((1 - way if late else way) * zh, zh)
        i = s + 2 if late else s - 1
        src = zg.at[zz(sign * (5 - s)), cut]
        return remote(src, zr.at[way, i], zr_send.at[way, i], zr_recv.at[way, i], dp, zz(sign) * NX + x)

    def zr_start(s, late):
        for way in range(2):
            zr_copy(s, way, late).start()

    def zr_next(s, late):
        for way in range(2):
            sign = 1 - 2 * way
            t = zz(sign * (4 - s))
            lo = (1 - way if late else way) * zh
            zr_copy(s, way, late).wait_recv()
            zg[t, lo:lo + zh] = zg[t, lo:lo + zh] + zr[way, s + 2 if late else s - 1]
            if s < 4:
                zr_copy(s + 1, way, late).start()

    def x_rows(to):
        return pl.ds(pl.multiple_of(16 * to, 16), 16)

    def zx_start():
        for r in range(1, NX):
            to = (x + r) % NX
            remote(zg.at[z, x_rows(to)], zx.at[r - 1], zx_send, zx_recv, dp, z * NX + to).start()

    def zx_last():
        pltpu.make_async_copy(zx, zx, zx_recv).wait()
        left_ref[2] = zg[z, x_rows(x)] + zx[0] + zx[1] + zx[2]

    def make_perm():
        p = lax.broadcasted_iota(jnp.int32, (NX * T, NX * T), 0)
        q = lax.broadcasted_iota(jnp.int32, (NX * T, NX * T), 1)
        place = ((p // 16) % NZ) * (16 * NX) + (p // T) * 16 + p % 16
        perm[...] = (place == q).astype(F32).astype(BF16)

    def make_table():
        load_owners.wait()
        lane = lax.broadcasted_iota(jnp.int32, (8, T), 1)
        lane_owner = (lane * 43) >> 8
        lane_rank = lane - lane_owner * CAP
        seen = jnp.zeros((8, T), jnp.int32)
        found = jnp.zeros((8, T), jnp.int32)
        mine = jnp.int32(0)
        for b in range(NMP):
            o = own[0, b]
            same = lane_owner == o
            found = jnp.where(same & (seen == lane_rank), b, found)
            seen = seen + same.astype(jnp.int32)
            mine = mine + (o == dp).astype(jnp.int32)
        tabv[...] = (found - mp + NMP) % NMP
        cp = pltpu.make_async_copy(tabv, tab, tab_sem)
        cp.start()
        cp.wait()
        return [jnp.where(k < mine, F32(0), F32(jnp.nan)) for k in range(CAP)]

    def right_out(k, empty):
        lo, n = CHUNK[k]
        r3 = (r3a, r3b)[k]
        for d in range(NT):
            @pl.when(dp != d)
            def _():
                pltpu.make_async_copy(r3.at[d], r3.at[d], r3_recv.at[k, d]).wait()

        first = (RPM * mp + lo) // T
        last = (RPM * mp + lo + n - 1) // T
        row = lax.broadcasted_iota(jnp.int32, (n, T), 0) + (RPM * mp + lo)
        upper = row < last * T
        for g in range(NT):
            one = (g + first) % NT
            two = (g + last) % NT
            for s in range(CAP):
                cut = slice(n * s, n * (s + 1))
                value = jnp.where(upper, r3[one, cut, :], r3[two, cut, :])
                right_ref[s, lo:lo + n, g * T:(g + 1) * T] = value + empty[s]

    def sent_early():
        for i in range(NY):
            @pl.when(has(order[i], other))
            def _():
                ra_copy(i).wait_send()

        @pl.when(has(q2, c))
        def _():
            rb_copy(0, 0).wait_send()
            rb_copy(0, 1).wait_send()

        for way in range(2):
            @pl.when(has((q1, q3)[way], c))
            def _():
                rb_copy(1, way).wait_send()
                rb_copy(2, way).wait_send()

        for l in range(2):
            for step in range(3):
                def done(n):
                    lx_copy(l, step, 0, n).wait_send()
                    lx_copy(l, step, 1, n).wait_send()

                by_parity(x + 4 - l + (0 if step == 0 else 1), done)
        for way in range(2):
            for s in range(1, 5):
                zr_copy(s, way, False).wait_send()
                if s > 1:
                    zr_copy(s, way, True).wait_send()

    def sent_late():
        for i in range(4):
            lz_copy(i).wait_send()
        sent = fin.at[pl.ds(1, 19)]
        pltpu.make_async_copy(sent, sent, fin_send).wait()
        pltpu.make_async_copy(zx, zx, zx_send).wait()

        @pl.when(active)
        def _():
            for k in range(2):
                sent = (r2a, r2b)[k].at[pl.ds(1, NMP - 1)]
                pltpu.make_async_copy(sent, sent, r2_send.at[k]).wait()
                for i in range(1, NDP):
                    r3_copy(k, i).wait_send()

    for l in (2, 0, 1):
        load_h[l].wait()
        for q in range(4):
            right_part(l, q)
    pl.semaphore_wait(barrier, NMP - 1 + NDP - 1)
    for i in range(4):
        ra_go(i)
    z_part()
    zr_start(1, False)
    zr_start(2, True)
    left_part(0)
    lx_start(0, 0)
    lx_start(0, 1)
    ra_sum(0)
    ra_sum(1)
    ra_sum(2)
    left_part(1)
    zr_next(1, False)
    lx_second(0)
    lx_start(1, 0)
    lx_start(1, 1)
    zr_next(2, True)
    ra_sum(3)
    empty = make_table()
    rb_second()
    zr_next(2, False)
    zr_next(3, True)
    lz_put(0)
    zr_next(3, False)
    lx_second(1)
    right_whole()
    r2_go(0)
    zr_next(4, True)
    zr_next(4, False)
    zx_start()
    lz_put(1)
    r2_go(1)
    lz_first()
    make_perm()
    sent_early()
    zx_last()
    r3_go(0)
    lz_second()
    r3_go(1)
    right_out(0, empty)
    lz_last()
    right_out(1, empty)
    sent_late()


def per_device(gradient, owners, left_old, right_old):
    rows = gradient.shape[0]
    dma = pltpu.SemaphoreType.DMA
    na, nb = CHUNK[0][1], CHUNK[1][1]
    left_gram, right_gram = pl.pallas_call(
        kernel,
        out_shape=(
            jax.ShapeDtypeStruct((3, 16, 512), F32),
            jax.ShapeDtypeStruct((CAP, RPM, RB), F32),
        ),
        in_specs=[
            pl.BlockSpec(memory_space=pl.ANY),
            pl.BlockSpec(memory_space=pl.ANY),
        ],
        out_specs=(
            pl.BlockSpec(memory_space=pltpu.VMEM),
            pl.BlockSpec(memory_space=pltpu.VMEM),
        ),
        scratch_shapes=[
            pltpu.VMEM((rows, RB), BF16),
            pltpu.VMEM((2, NX, NZ, 16, RB), BF16),
            pltpu.VMEM((NDP, 4, T, T), F32),
            pltpu.VMEM((NY, 4, T, T), F32),
            pltpu.VMEM((2, 2, T, T), F32),
            pltpu.VMEM((2, 4, T, T), F32),
            pltpu.VMEM((RB, T), F32),
            pltpu.VMEM((NMP, RPM, T), F32),
            pltpu.VMEM((NMP, na, T), F32),
            pltpu.VMEM((NMP, nb, T), F32),
            pltpu.VMEM((NDP, CAP * na, T), F32),
            pltpu.VMEM((NDP, CAP * nb, T), F32),
            pltpu.VMEM((NDP, CAP * na, T), F32),
            pltpu.VMEM((NDP, CAP * nb, T), F32),
            pltpu.VMEM((2, 4, 3, T, T), F32),
            pltpu.VMEM((2, 2, 3, T // 2, T), F32),
            pltpu.VMEM((2, 2, 3, T, T), F32),
            pltpu.VMEM((NZ, 4, 2, 16, T), F32),
            pltpu.VMEM((2, 4, 2, 16, T), F32),
            pltpu.VMEM((2, 2, 2, 16, T), F32),
            pltpu.VMEM((20, 2, 16, T), F32),
            pltpu.VMEM((NZ, 16 * NX, NX * T), F32),
            pltpu.VMEM((2, 7, 8 * NX, NX * T), F32),
            pltpu.VMEM((3, 16, NX * T), F32),
            pltpu.VMEM((4 * T, 4 * T), BF16),
            pltpu.SMEM((1, NMP), jnp.int32),
            pltpu.VMEM((8, T), jnp.int32),
            pltpu.SMEM((8, T), jnp.int32),
            dma((4,)), dma,
            dma((NY,)), dma((NY,)), dma((6,)), dma((6,)),
            dma((2,)), dma((2,)), dma((2, NDP)), dma((2, NDP)),
            dma((2, 6)), dma((2, 6)), dma((4,)), dma((4,)), dma, dma,
            dma((2, 7)), dma((2, 7)), dma, dma,
        ],
        compiler_params=pltpu.CompilerParams(
            collective_id=0, has_side_effects=True, vmem_limit_bytes=105 * 512 * 1024
        ),
        name="stats",
    )(gradient, owners.reshape(1, NMP))
    left_stats = BETA * left_old + left_gram
    right_stats = jnp.where(jnp.isnan(right_gram), 0.0, BETA * right_old + right_gram)
    return left_stats, right_stats


def solution(mesh):
    in_specs = (P("dp", "mp"), P(), P("dp", "mp", None), P("dp", "mp", None))
    out_specs = (P("dp", "mp", None), P("dp", "mp", None))
    return jax.shard_map(
        per_device, mesh=mesh, in_specs=in_specs, out_specs=out_specs, check_vma=False
    )
```

```python
import jax
import jax.numpy as jnp
from jax import lax
from jax.experimental import pallas as pl
from jax.experimental.pallas import tpu as pltpu
from jax.sharding import PartitionSpec as P

BETA = 0.95
F32 = jnp.float32
BF16 = jnp.bfloat16
RB = 896
T = 128
NT = 7
NMP = 32
NDP = 8
CAP = 6
RPM = 28
NY = 4
NX = 4
NZ = 8

CHUNK = ((0, 16), (16, 12))

LEFT_TILES = (
    ((0, 0), (2, 2), (1, 3)),
    ((0, 1), (2, 3)),
    ((1, 1), (3, 3), (2, 0)),
    ((0, 3), (2, 1)),
)


def remote(src, dst, send_sem, recv_sem, dp, mp):
    return pltpu.make_async_remote_copy(
        src_ref=src,
        dst_ref=dst,
        send_sem=send_sem,
        recv_sem=recv_sem,
        device_id=(dp, mp),
        device_id_type=pl.DeviceIdType.MESH,
    )


def kernel(
    grad_ref, owners_ref, left_ref, right_ref,
    h, a, part, ra, rb1, rb2, tall, t28, r2a, r2b, s3a, s3b, r3a, r3b,
    lp, lx1, lx2, lz, rly, rlyh, fin, zg, zr, zx, perm, own, tabv, tab,
    in_sem, tab_sem, ra_send, ra_recv, rb_send, rb_recv,
    r2_send, r2_recv, r3_send, r3_recv,
    lx_send, lx_recv, lz_send, lz_recv, fin_send, fin_recv,
    zr_send, zr_recv, zx_send, zx_recv,
):
    dp = lax.axis_index("dp")
    mp = lax.axis_index("mp")
    y, c = dp // 2, dp % 2
    z, x = mp // NX, mp % NX
    other = 1 - c
    half = T // 2
    xs = (z * NX + (x + 1) % NX, z * NX + (x + 3) % NX)
    ys = (2 * ((y + 1) % NY) + c, 2 * ((y + 3) % NY) + c)
    active = dp < NT

    def has(q, core):
        return 2 * q + core < NT

    nb = NX * T
    load_h = {}
    for l in (2, 0, 1):
        load_h[l] = pltpu.make_async_copy(grad_ref.at[pl.ds(l * nb, nb)], h.at[pl.ds(l * nb, nb)], in_sem.at[l])
        load_h[l].start()
    load_owners = pltpu.make_async_copy(owners_ref, own, in_sem.at[3])
    load_owners.start()

    barrier = pltpu.get_barrier_semaphore()

    def hello_mp(i, carry):
        pl.semaphore_signal(barrier, inc=1, device_id=(dp, (mp + i) % NMP), device_id_type=pl.DeviceIdType.MESH)
        return carry

    def hello_dp(i, carry):
        pl.semaphore_signal(barrier, inc=1, device_id=((dp + i) % NDP, mp), device_id_type=pl.DeviceIdType.MESH)
        return carry

    lax.fori_loop(1, NDP, hello_dp, 0)
    lax.fori_loop(1, NMP, hello_mp, 0)

    def right_part(l, q):
        lo = 2 * T * q
        wide = min(2 * T, RB - lo)
        some = slice(l * nb, (l + 1) * nb)
        block = lax.dot_general(
            h[some, lo:RB], h[some, lo:lo + wide], (((0,), (0,)), ((), ())), preferred_element_type=F32
        )
        for col in range(2 * q, 2 * q + wide // T):
            for row in range(col, NT):
                d = (row + col) % NT
                u = (4 * d) % NT
                k = min((row - u) % NT, (u - row) % NT)
                i, j = (row - 2 * q) * T, (col - 2 * q) * T
                tile = block[i:i + T, j:j + T]
                part[d, k] = tile if l == 2 else part[d, k] + tile

    order = [(y + k) % NY for k in (2, 1, 3, 0)]
    q2, q1, q3, q0 = order

    def ra_copy(i):
        q = order[i]
        return remote(part.at[2 * q + other], ra.at[q], ra_send.at[i], ra_recv.at[i], dp + 1 - 2 * c, mp)

    def ra_go(i):
        @pl.when(has(order[i], other))
        def _():
            ra_copy(i).start()

    def rb_copy(step, way):
        i = 2 * step + way
        tiles = pl.ds(2 * way, 2) if step != 1 else pl.ds(2 - 2 * way, 2)
        q = (q2, (q1, q3)[way], (q1, q3)[way])[step]
        dst = rb1.at[way] if step == 0 else rb2.at[way, tiles]
        return remote(part.at[2 * q + c, tiles], dst, rb_send.at[i], rb_recv.at[i], ys[way], mp)

    def ra_sum(i):
        q = order[i]

        @pl.when(has(q, c))
        def _():
            ra_copy(i).wait_recv()
            part[2 * q + c] = part[2 * q + c] + ra[q]
            if i == 0:
                rb_copy(0, 0).start()
                rb_copy(0, 1).start()
            elif i < 3:
                rb_copy(1, i - 1).start()

    def rb_second():
        for way in range(2):
            q = (q1, q3)[way]

            @pl.when(has(q, c))
            def _():
                rb_copy(0, way).wait_recv()
                t = 2 * q + c
                part[t, 2 * way:2 * way + 2] = part[t, 2 * way:2 * way + 2] + rb1[way]
                rb_copy(2, way).start()

    def right_whole():
        @pl.when(active)
        def _():
            for way in range(2):
                rb_copy(1, way).wait_recv()
                rb_copy(2, way).wait_recv()
            u = (4 * dp) % NT
            for k in range(4):
                tile = part[dp, k] + rb2[0, k] + rb2[1, k]
                one = (u + k) % NT
                two = (u + NT - k) % NT
                if k == 0:
                    tall[pl.ds(pl.multiple_of(one * T, T), T), :] = tile
                else:
                    big = jnp.maximum(one, two)
                    small = jnp.minimum(one, two)
                    tall[pl.ds(pl.multiple_of(big * T, T), T), :] = tile
                    tall[pl.ds(pl.multiple_of(small * T, T), T), :] = tile.T
            for m in range(NMP):
                t28[m] = tall[RPM * m:RPM * (m + 1)]

    def r2_go(k):
        lo, n = CHUNK[k]
        r2 = (r2a, r2b)[k]

        @pl.when(active)
        def _():
            for i in range(1, NMP):
                to = (mp + i) % NMP
                remote(t28.at[to, pl.ds(lo, n)], r2.at[NMP - i], r2_send.at[k], r2_recv.at[k], dp, to).start()
            r2[0] = t28[mp, lo:lo + n]

    def r3_copy(k, i):
        o = (dp + i) % NDP
        s3, r3 = ((s3a, r3a), (s3b, r3b))[k]
        return remote(s3.at[o], r3.at[dp], r3_send.at[k, i], r3_recv.at[k, dp], o, mp)

    def r3_go(k):
        n = CHUNK[k][1]
        s3, r3 = ((s3a, r3a), (s3b, r3b))[k]
        r2 = (r2a, r2b)[k]

        @pl.when(active)
        def _():
            everything = r2.at[pl.ds(1, NMP - 1)]
            pltpu.make_async_copy(everything, everything, r2_recv.at[k]).wait()
            for o in range(NDP):
                for s in range(CAP):
                    s3[o, n * s:n * (s + 1), :] = r2[tab[0, o * CAP + s]]
            for i in range(1, NDP):
                r3_copy(k, i).start()
            r3[dp] = s3[dp]

    def left_part(l):
        for g in range(NX):
            for i in range(NZ):
                lo = NX * T * l + 16 * NX * i + 16 * g
                a[l, g, i] = h[lo:lo + 16, :]
        g = a[l].reshape(NX * T, RB)
        block = lax.dot_general(g, g, (((1,), (1,)), ((), ())), preferred_element_type=F32)
        for v in range(4):
            for i, (r, s) in enumerate(LEFT_TILES[v]):
                lp[l, v, i] = block[r * T:(r + 1) * T, s * T:(s + 1) * T]

    def by_parity(value, fn):
        @pl.when(value % 2 == 0)
        def _():
            fn(3)

        @pl.when(value % 2 == 1)
        def _():
            fn(2)

    def lx_copy(l, step, way, n):
        i = 2 * step + way
        v = ((x + 2, x + 1, x + 1), (x + 2, x + 3, x + 3))[way][step]
        v = (v + 4 - l) % 4
        lo = half * way if step != 1 else half * (1 - way)
        tiles = pl.ds(0, n)
        part_rows = pl.ds(lo, half)
        dst = lx1.at[l, way, tiles] if step == 0 else lx2.at[l, way, tiles, part_rows]
        src = lp.at[l, v, tiles, part_rows]
        return remote(src, dst, lx_send.at[l, i], lx_recv.at[l, i], dp, xs[way])

    def lx_start(l, step):
        def go(n):
            lx_copy(l, step, 0, n).start()
            lx_copy(l, step, 1, n).start()

        by_parity(x + 4 - l + (0 if step == 0 else 1), go)

    def lx_second(l):
        def go(n):
            for way in range(2):
                lx_copy(l, 0, way, n).wait_recv()
                v = (x + (1, 3)[way] + 4 - l) % 4
                cut = slice(half * way, half * (way + 1))
                lp[l, v, :n, cut] = lp[l, v, :n, cut] + lx1[l, way, :n]
                lx_copy(l, 2, way, n).start()

        by_parity(x + 1 + 4 - l, go)

    def zz(k):
        return (z + NZ + k) % NZ

    def lz_copy(i):
        to, src, dst = (
            (1, lz.at[zz(3)], rly.at[0]),
            (-1, lz.at[zz(-3)], rly.at[1]),
            (2, lz.at[zz(4), pl.ds(0, 2)], rlyh.at[0]),
            (-2, lz.at[zz(4), pl.ds(2, 2)], rlyh.at[1]),
        )[i]
        return remote(src, dst, lz_send.at[i], lz_recv.at[i], dp, zz(to) * NX + x)

    hops = (0, 1, -1, 2, -2)

    def fin_start(j):
        for r in range(0 if j else 1, 4):
            g = (x + 4 - r) % 4
            to = zz(hops[j])
            remote(lz.at[to, g], fin.at[4 * j + r], fin_send, fin_recv, dp, to * NX + g).start()

    def lz_put(l):
        def go(n):
            for way in range(2):
                lx_copy(l, 1, way, n).wait_recv()
                lx_copy(l, 2, way, n).wait_recv()
            v = (x + 4 - l) % 4
            tiles = [lp[l, v, i] + lx2[l, 0, i] + lx2[l, 1, i] for i in range(n)]

            def put(g, tile):
                lz[:, g, l] = tile.reshape(NZ, 16, T)

            if n == 3:
                w = v // 2
                put(w, tiles[0])
                put(w + 2, tiles[1])
                put(w + 1, tiles[2])
                put((w + 3) % 4, tiles[2].T)
            else:
                put(0, tiles[0])
                put(v, tiles[0].T)
                put(2, tiles[1])
                put((v + 2) % 4, tiles[1].T)

        by_parity(x + 4 - l, go)

    def lz_first():
        for i in (2, 3, 0, 1):
            lz_copy(i).start()
        for j in (1, 2, 0):
            fin_start(j)
        fin[0] = lz[z, x]

    def lz_second():
        for way in range(2):
            t = (zz(2), zz(-2))[way]
            lz_copy(way).wait_recv()
            lz_copy(2 + way).wait_recv()
            lz[t] = lz[t] + rly[way]
            lz[t, 2 * way:2 * way + 2] = lz[t, 2 * way:2 * way + 2] + rlyh[way]
            fin_start(3 + way)

    def lz_last():
        everything = fin.at[pl.ds(1, 19)]
        pltpu.make_async_copy(everything, everything, fin_recv).wait()
        rows = []
        for l in range(2):
            row = []
            for g in range(4):
                r = (g + l) % 4
                row.append(fin[r, l] + fin[4 + r, l] + fin[8 + r, l] + fin[12 + r, l] + fin[16 + r, l])
            rows.append(jnp.concatenate(row, axis=1))
        rows = jnp.concatenate(rows, axis=0)
        total = None
        for _ in range(3):
            piece = rows.astype(BF16)
            rows = rows - piece.astype(F32)
            term = jnp.dot(piece, perm[...], preferred_element_type=F32)
            total = term if total is None else total + term
        left_ref[0] = total[:16]
        left_ref[1] = total[16:]

    zh = 8 * NX

    def z_part():
        g = h[2 * NX * T:3 * NX * T, :]
        block = lax.dot_general(g, g, (((1,), (1,)), ((), ())), preferred_element_type=F32)
        zg[...] = block.reshape(NZ, 16 * NX, NX * T)

    def zr_copy(s, way, late):
        sign = 1 - 2 * way
        cut = pl.ds((1 - way if late else way) * zh, zh)
        i = s + 2 if late else s - 1
        src = zg.at[zz(sign * (5 - s)), cut]
        return remote(src, zr.at[way, i], zr_send.at[way, i], zr_recv.at[way, i], dp, zz(sign) * NX + x)

    def zr_start(s, late):
        for way in range(2):
            zr_copy(s, way, late).start()

    def zr_next(s, late):
        for way in range(2):
            sign = 1 - 2 * way
            t = zz(sign * (4 - s))
            lo = (1 - way if late else way) * zh
            zr_copy(s, way, late).wait_recv()
            zg[t, lo:lo + zh] = zg[t, lo:lo + zh] + zr[way, s + 2 if late else s - 1]
            if s < 4:
                zr_copy(s + 1, way, late).start()

    def x_rows(to):
        return pl.ds(pl.multiple_of(16 * to, 16), 16)

    def zx_start():
        for r in range(1, NX):
            to = (x + r) % NX
            remote(zg.at[z, x_rows(to)], zx.at[r - 1], zx_send, zx_recv, dp, z * NX + to).start()

    def zx_last():
        pltpu.make_async_copy(zx, zx, zx_recv).wait()
        left_ref[2] = zg[z, x_rows(x)] + zx[0] + zx[1] + zx[2]

    def make_perm():
        p = lax.broadcasted_iota(jnp.int32, (NX * T, NX * T), 0)
        q = lax.broadcasted_iota(jnp.int32, (NX * T, NX * T), 1)
        place = ((p // 16) % NZ) * (16 * NX) + (p // T) * 16 + p % 16
        perm[...] = (place == q).astype(F32).astype(BF16)

    def make_table():
        load_owners.wait()
        lane = lax.broadcasted_iota(jnp.int32, (8, T), 1)
        lane_owner = (lane * 43) >> 8
        lane_rank = lane - lane_owner * CAP
        seen = jnp.zeros((8, T), jnp.int32)
        found = jnp.zeros((8, T), jnp.int32)
        mine = jnp.int32(0)
        for b in range(NMP):
            o = own[0, b]
            same = lane_owner == o
            found = jnp.where(same & (seen == lane_rank), b, found)
            seen = seen + same.astype(jnp.int32)
            mine = mine + (o == dp).astype(jnp.int32)
        tabv[...] = (found - mp + NMP) % NMP
        cp = pltpu.make_async_copy(tabv, tab, tab_sem)
        cp.start()
        cp.wait()
        return [jnp.where(k < mine, F32(0), F32(jnp.nan)) for k in range(CAP)]

    def right_out(k, empty):
        lo, n = CHUNK[k]
        r3 = (r3a, r3b)[k]
        for d in range(NT):
            @pl.when(dp != d)
            def _():
                pltpu.make_async_copy(r3.at[d], r3.at[d], r3_recv.at[k, d]).wait()

        first = (RPM * mp + lo) // T
        last = (RPM * mp + lo + n - 1) // T
        row = lax.broadcasted_iota(jnp.int32, (n, T), 0) + (RPM * mp + lo)
        upper = row < last * T
        for g in range(NT):
            one = (g + first) % NT
            two = (g + last) % NT
            for s in range(CAP):
                cut = slice(n * s, n * (s + 1))
                value = jnp.where(upper, r3[one, cut, :], r3[two, cut, :])
                right_ref[s, lo:lo + n, g * T:(g + 1) * T] = value + empty[s]

    def sent_early():
        for i in range(NY):
            @pl.when(has(order[i], other))
            def _():
                ra_copy(i).wait_send()

        @pl.when(has(q2, c))
        def _():
            rb_copy(0, 0).wait_send()
            rb_copy(0, 1).wait_send()

        for way in range(2):
            @pl.when(has((q1, q3)[way], c))
            def _():
                rb_copy(1, way).wait_send()
                rb_copy(2, way).wait_send()

        for l in range(2):
            for step in range(3):
                def done(n):
                    lx_copy(l, step, 0, n).wait_send()
                    lx_copy(l, step, 1, n).wait_send()

                by_parity(x + 4 - l + (0 if step == 0 else 1), done)
        for way in range(2):
            for s in range(1, 5):
                zr_copy(s, way, False).wait_send()
                if s > 1:
                    zr_copy(s, way, True).wait_send()

    def sent_next():
        for i in range(4):
            lz_copy(i).wait_send()
        pltpu.make_async_copy(zx, zx, zx_send).wait()

        @pl.when(active)
        def _():
            for k in range(2):
                sent = (r2a, r2b)[k].at[pl.ds(1, NMP - 1)]
                pltpu.make_async_copy(sent, sent, r2_send.at[k]).wait()
            for i in range(1, NDP):
                r3_copy(0, i).wait_send()

    def sent_late():
        sent = fin.at[pl.ds(1, 19)]
        pltpu.make_async_copy(sent, sent, fin_send).wait()

        @pl.when(active)
        def _():
            for i in range(1, NDP):
                r3_copy(1, i).wait_send()

    for l in (2, 0, 1):
        load_h[l].wait()
        for q in range(4):
            right_part(l, q)
    pl.semaphore_wait(barrier, NMP - 1 + NDP - 1)
    for i in range(4):
        ra_go(i)
    z_part()
    zr_start(1, False)
    zr_start(2, True)
    left_part(0)
    lx_start(0, 0)
    lx_start(0, 1)
    ra_sum(0)
    ra_sum(1)
    ra_sum(2)
    zr_next(1, False)
    left_part(1)
    lx_second(0)
    lx_start(1, 0)
    lx_start(1, 1)
    zr_next(2, True)
    ra_sum(3)
    rb_second()
    zr_next(2, False)
    zr_next(3, True)
    lz_put(0)
    zr_next(3, False)
    lx_second(1)
    empty = make_table()
    make_perm()
    right_whole()
    r2_go(0)
    zr_next(4, True)
    zr_next(4, False)
    zx_start()
    r2_go(1)
    lz_put(1)
    lz_first()
    r3_go(0)
    sent_early()
    zx_last()
    r3_go(1)
    lz_second()
    right_out(0, empty)
    sent_next()
    lz_last()
    right_out(1, empty)
    sent_late()


def per_device(gradient, owners, left_old, right_old):
    rows = gradient.shape[0]
    dma = pltpu.SemaphoreType.DMA
    na, nb = CHUNK[0][1], CHUNK[1][1]
    left_gram, right_gram = pl.pallas_call(
        kernel,
        out_shape=(
            jax.ShapeDtypeStruct((3, 16, 512), F32),
            jax.ShapeDtypeStruct((CAP, RPM, RB), F32),
        ),
        in_specs=[
            pl.BlockSpec(memory_space=pl.ANY),
            pl.BlockSpec(memory_space=pl.ANY),
        ],
        out_specs=(
            pl.BlockSpec(memory_space=pltpu.VMEM),
            pl.BlockSpec(memory_space=pltpu.VMEM),
        ),
        scratch_shapes=[
            pltpu.VMEM((rows, RB), BF16),
            pltpu.VMEM((2, NX, NZ, 16, RB), BF16),
            pltpu.VMEM((NDP, 4, T, T), F32),
            pltpu.VMEM((NY, 4, T, T), F32),
            pltpu.VMEM((2, 2, T, T), F32),
            pltpu.VMEM((2, 4, T, T), F32),
            pltpu.VMEM((RB, T), F32),
            pltpu.VMEM((NMP, RPM, T), F32),
            pltpu.VMEM((NMP, na, T), F32),
            pltpu.VMEM((NMP, nb, T), F32),
            pltpu.VMEM((NDP, CAP * na, T), F32),
            pltpu.VMEM((NDP, CAP * nb, T), F32),
            pltpu.VMEM((NDP, CAP * na, T), F32),
            pltpu.VMEM((NDP, CAP * nb, T), F32),
            pltpu.VMEM((2, 4, 3, T, T), F32),
            pltpu.VMEM((2, 2, 3, T // 2, T), F32),
            pltpu.VMEM((2, 2, 3, T, T), F32),
            pltpu.VMEM((NZ, 4, 2, 16, T), F32),
            pltpu.VMEM((2, 4, 2, 16, T), F32),
            pltpu.VMEM((2, 2, 2, 16, T), F32),
            pltpu.VMEM((20, 2, 16, T), F32),
            pltpu.VMEM((NZ, 16 * NX, NX * T), F32),
            pltpu.VMEM((2, 7, 8 * NX, NX * T), F32),
            pltpu.VMEM((3, 16, NX * T), F32),
            pltpu.VMEM((4 * T, 4 * T), BF16),
            pltpu.SMEM((1, NMP), jnp.int32),
            pltpu.VMEM((8, T), jnp.int32),
            pltpu.SMEM((8, T), jnp.int32),
            dma((4,)), dma,
            dma((NY,)), dma((NY,)), dma((6,)), dma((6,)),
            dma((2,)), dma((2,)), dma((2, NDP)), dma((2, NDP)),
            dma((2, 6)), dma((2, 6)), dma((4,)), dma((4,)), dma, dma,
            dma((2, 7)), dma((2, 7)), dma, dma,
        ],
        compiler_params=pltpu.CompilerParams(
            collective_id=0, has_side_effects=True, vmem_limit_bytes=105 * 512 * 1024
        ),
        name="stats",
    )(gradient, owners.reshape(1, NMP))
    left_stats = BETA * left_old + left_gram
    right_stats = jnp.where(jnp.isnan(right_gram), 0.0, BETA * right_old + right_gram)
    return left_stats, right_stats


def solution(mesh):
    in_specs = (P("dp", "mp"), P(), P("dp", "mp", None), P("dp", "mp", None))
    out_specs = (P("dp", "mp", None), P("dp", "mp", None))
    return jax.shard_map(
        per_device, mesh=mesh, in_specs=in_specs, out_specs=out_specs, check_vma=False
    )
```

```python
import jax
import jax.numpy as jnp
from jax import lax
from jax.experimental import pallas as pl
from jax.experimental.pallas import tpu as pltpu
from jax.sharding import PartitionSpec as P

BETA = 0.95
F32 = jnp.float32
BF16 = jnp.bfloat16
RB = 896
T = 128
NT = 7
NMP = 32
NDP = 8
CAP = 6
RPM = 28
NY = 4
NX = 4
NZ = 8

CHUNK = ((0, 16), (16, 12))

LEFT_TILES = (
    ((0, 0), (2, 2), (1, 3)),
    ((0, 1), (2, 3)),
    ((1, 1), (3, 3), (2, 0)),
    ((0, 3), (2, 1)),
)


def remote(src, dst, send_sem, recv_sem, dp, mp):
    return pltpu.make_async_remote_copy(
        src_ref=src,
        dst_ref=dst,
        send_sem=send_sem,
        recv_sem=recv_sem,
        device_id=(dp, mp),
        device_id_type=pl.DeviceIdType.MESH,
    )


def kernel(
    grad_ref, owners_ref, left_ref, right_ref,
    h, a, part, ra, rb1, rb2, tall, t28, r2a, r2b, s3a, s3b, r3a, r3b,
    lp, lx1, lx2, lz, rly, rlyh, fin, zg, zr, zx, perm, own, tabv, tab,
    in_sem, tab_sem, ra_send, ra_recv, rb_send, rb_recv,
    r2_send, r2_recv, r3_send, r3_recv,
    lx_send, lx_recv, lz_send, lz_recv, fin_send, fin_recv,
    zr_send, zr_recv, zx_send, zx_recv,
):
    dp = lax.axis_index("dp")
    mp = lax.axis_index("mp")
    y, c = dp // 2, dp % 2
    z, x = mp // NX, mp % NX
    other = 1 - c
    half = T // 2
    xs = (z * NX + (x + 1) % NX, z * NX + (x + 3) % NX)
    ys = (2 * ((y + 1) % NY) + c, 2 * ((y + 3) % NY) + c)
    active = dp < NT

    def has(q, core):
        return 2 * q + core < NT

    nb = NX * T
    load_h = {}
    for l in (2, 0, 1):
        load_h[l] = pltpu.make_async_copy(grad_ref.at[pl.ds(l * nb, nb)], h.at[pl.ds(l * nb, nb)], in_sem.at[l])
        load_h[l].start()
    load_owners = pltpu.make_async_copy(owners_ref, own, in_sem.at[3])
    load_owners.start()

    barrier = pltpu.get_barrier_semaphore()

    def hello_mp(i, carry):
        pl.semaphore_signal(barrier, inc=1, device_id=(dp, (mp + i) % NMP), device_id_type=pl.DeviceIdType.MESH)
        return carry

    def hello_dp(i, carry):
        pl.semaphore_signal(barrier, inc=1, device_id=((dp + i) % NDP, mp), device_id_type=pl.DeviceIdType.MESH)
        return carry

    lax.fori_loop(1, NDP, hello_dp, 0)
    lax.fori_loop(1, NMP, hello_mp, 0)

    def right_part(l, q):
        lo = 2 * T * q
        wide = min(2 * T, RB - lo)
        some = slice(l * nb, (l + 1) * nb)
        block = lax.dot_general(
            h[some, lo:RB], h[some, lo:lo + wide], (((0,), (0,)), ((), ())), preferred_element_type=F32
        )
        for col in range(2 * q, 2 * q + wide // T):
            for row in range(col, NT):
                d = (row + col) % NT
                u = (4 * d) % NT
                k = min((row - u) % NT, (u - row) % NT)
                i, j = (row - 2 * q) * T, (col - 2 * q) * T
                tile = block[i:i + T, j:j + T]
                part[d, k] = tile if l == 2 else part[d, k] + tile

    order = [(y + k) % NY for k in (2, 1, 3, 0)]
    q2, q1, q3, q0 = order

    def ra_copy(i):
        q = order[i]
        return remote(part.at[2 * q + other], ra.at[q], ra_send.at[i], ra_recv.at[i], dp + 1 - 2 * c, mp)

    def ra_go(i):
        @pl.when(has(order[i], other))
        def _():
            ra_copy(i).start()

    def rb_copy(step, way):
        i = 2 * step + way
        tiles = pl.ds(2 * way, 2) if step != 1 else pl.ds(2 - 2 * way, 2)
        q = (q2, (q1, q3)[way], (q1, q3)[way])[step]
        dst = rb1.at[way] if step == 0 else rb2.at[way, tiles]
        return remote(part.at[2 * q + c, tiles], dst, rb_send.at[i], rb_recv.at[i], ys[way], mp)

    def ra_sum(i):
        q = order[i]

        @pl.when(has(q, c))
        def _():
            ra_copy(i).wait_recv()
            part[2 * q + c] = part[2 * q + c] + ra[q]
            if i == 0:
                rb_copy(0, 0).start()
                rb_copy(0, 1).start()
            elif i < 3:
                rb_copy(1, i - 1).start()

    def rb_second():
        for way in range(2):
            q = (q1, q3)[way]

            @pl.when(has(q, c))
            def _():
                rb_copy(0, way).wait_recv()
                t = 2 * q + c
                part[t, 2 * way:2 * way + 2] = part[t, 2 * way:2 * way + 2] + rb1[way]
                rb_copy(2, way).start()

    def right_whole():
        @pl.when(active)
        def _():
            for way in range(2):
                rb_copy(1, way).wait_recv()
                rb_copy(2, way).wait_recv()
            u = (4 * dp) % NT
            for k in range(4):
                tile = part[dp, k] + rb2[0, k] + rb2[1, k]
                one = (u + k) % NT
                two = (u + NT - k) % NT
                if k == 0:
                    tall[pl.ds(pl.multiple_of(one * T, T), T), :] = tile
                else:
                    big = jnp.maximum(one, two)
                    small = jnp.minimum(one, two)
                    tall[pl.ds(pl.multiple_of(big * T, T), T), :] = tile
                    tall[pl.ds(pl.multiple_of(small * T, T), T), :] = tile.T
            for m in range(NMP):
                t28[m] = tall[RPM * m:RPM * (m + 1)]

    def r2_go(k):
        lo, n = CHUNK[k]
        r2 = (r2a, r2b)[k]

        @pl.when(active)
        def _():
            for i in range(1, NMP):
                to = (mp + i) % NMP
                remote(t28.at[to, pl.ds(lo, n)], r2.at[NMP - i], r2_send.at[k], r2_recv.at[k], dp, to).start()
            r2[0] = t28[mp, lo:lo + n]

    def r3_copy(k, i):
        o = (dp + i) % NDP
        s3, r3 = ((s3a, r3a), (s3b, r3b))[k]
        return remote(s3.at[o], r3.at[dp], r3_send.at[k, i], r3_recv.at[k, dp], o, mp)

    def r3_go(k):
        n = CHUNK[k][1]
        s3, r3 = ((s3a, r3a), (s3b, r3b))[k]
        r2 = (r2a, r2b)[k]

        @pl.when(active)
        def _():
            everything = r2.at[pl.ds(1, NMP - 1)]
            pltpu.make_async_copy(everything, everything, r2_recv.at[k]).wait()
            for o in range(NDP):
                for s in range(CAP):
                    s3[o, n * s:n * (s + 1), :] = r2[tab[0, o * CAP + s]]
            for i in range(1, NDP):
                r3_copy(k, i).start()
            r3[dp] = s3[dp]

    def left_part(l):
        for g in range(NX):
            for i in range(NZ):
                lo = NX * T * l + 16 * NX * i + 16 * g
                a[l, g, i] = h[lo:lo + 16, :]
        g = a[l].reshape(NX * T, RB)
        block = lax.dot_general(g, g, (((1,), (1,)), ((), ())), preferred_element_type=F32)
        for v in range(4):
            for i, (r, s) in enumerate(LEFT_TILES[v]):
                lp[l, v, i] = block[r * T:(r + 1) * T, s * T:(s + 1) * T]

    def by_parity(value, fn):
        @pl.when(value % 2 == 0)
        def _():
            fn(3)

        @pl.when(value % 2 == 1)
        def _():
            fn(2)

    def lx_copy(l, step, way, n):
        i = 2 * step + way
        v = ((x + 2, x + 1, x + 1), (x + 2, x + 3, x + 3))[way][step]
        v = (v + 4 - l) % 4
        lo = half * way if step != 1 else half * (1 - way)
        tiles = pl.ds(0, n)
        part_rows = pl.ds(lo, half)
        dst = lx1.at[l, way, tiles] if step == 0 else lx2.at[l, way, tiles, part_rows]
        src = lp.at[l, v, tiles, part_rows]
        return remote(src, dst, lx_send.at[l, i], lx_recv.at[l, i], dp, xs[way])

    def lx_start(l, step):
        def go(n):
            lx_copy(l, step, 0, n).start()
            lx_copy(l, step, 1, n).start()

        by_parity(x + 4 - l + (0 if step == 0 else 1), go)

    def lx_second(l):
        def go(n):
            for way in range(2):
                lx_copy(l, 0, way, n).wait_recv()
                v = (x + (1, 3)[way] + 4 - l) % 4
                cut = slice(half * way, half * (way + 1))
                lp[l, v, :n, cut] = lp[l, v, :n, cut] + lx1[l, way, :n]
                lx_copy(l, 2, way, n).start()

        by_parity(x + 1 + 4 - l, go)

    def zz(k):
        return (z + NZ + k) % NZ

    def lz_copy(i):
        to, src, dst = (
            (1, lz.at[zz(3)], rly.at[0]),
            (-1, lz.at[zz(-3)], rly.at[1]),
            (2, lz.at[zz(4), pl.ds(0, 2)], rlyh.at[0]),
            (-2, lz.at[zz(4), pl.ds(2, 2)], rlyh.at[1]),
        )[i]
        return remote(src, dst, lz_send.at[i], lz_recv.at[i], dp, zz(to) * NX + x)

    hops = (0, 1, -1, 2, -2)

    def fin_start(j):
        for r in range(0 if j else 1, 4):
            g = (x + 4 - r) % 4
            to = zz(hops[j])
            remote(lz.at[to, g], fin.at[4 * j + r], fin_send, fin_recv, dp, to * NX + g).start()

    def lz_put(l):
        def go(n):
            for way in range(2):
                lx_copy(l, 1, way, n).wait_recv()
                lx_copy(l, 2, way, n).wait_recv()
            v = (x + 4 - l) % 4
            tiles = [lp[l, v, i] + lx2[l, 0, i] + lx2[l, 1, i] for i in range(n)]

            def put(g, tile):
                lz[:, g, l] = tile.reshape(NZ, 16, T)

            if n == 3:
                w = v // 2
                put(w, tiles[0])
                put(w + 2, tiles[1])
                put(w + 1, tiles[2])
                put((w + 3) % 4, tiles[2].T)
            else:
                put(0, tiles[0])
                put(v, tiles[0].T)
                put(2, tiles[1])
                put((v + 2) % 4, tiles[1].T)

        by_parity(x + 4 - l, go)

    def lz_first():
        for i in (2, 3, 0, 1):
            lz_copy(i).start()
        for j in (1, 2, 0):
            fin_start(j)
        fin[0] = lz[z, x]

    def lz_second():
        for way in range(2):
            t = (zz(2), zz(-2))[way]
            lz_copy(way).wait_recv()
            lz_copy(2 + way).wait_recv()
            lz[t] = lz[t] + rly[way]
            lz[t, 2 * way:2 * way + 2] = lz[t, 2 * way:2 * way + 2] + rlyh[way]
            fin_start(3 + way)

    def lz_last():
        everything = fin.at[pl.ds(1, 19)]
        pltpu.make_async_copy(everything, everything, fin_recv).wait()
        rows = []
        for l in range(2):
            row = []
            for g in range(4):
                r = (g + l) % 4
                row.append(fin[r, l] + fin[4 + r, l] + fin[8 + r, l] + fin[12 + r, l] + fin[16 + r, l])
            rows.append(jnp.concatenate(row, axis=1))
        rows = jnp.concatenate(rows, axis=0)
        total = None
        for _ in range(3):
            piece = rows.astype(BF16)
            rows = rows - piece.astype(F32)
            term = jnp.dot(piece, perm[...], preferred_element_type=F32)
            total = term if total is None else total + term
        left_ref[0] = total[:16]
        left_ref[1] = total[16:]

    zh = 8 * NX

    def z_part():
        g = h[2 * NX * T:3 * NX * T, :]
        block = lax.dot_general(g, g, (((1,), (1,)), ((), ())), preferred_element_type=F32)
        zg[...] = block.reshape(NZ, 16 * NX, NX * T)

    def zr_copy(s, way, late):
        sign = 1 - 2 * way
        cut = pl.ds((1 - way if late else way) * zh, zh)
        i = s + 2 if late else s - 1
        src = zg.at[zz(sign * (5 - s)), cut]
        return remote(src, zr.at[way, i], zr_send.at[way, i], zr_recv.at[way, i], dp, zz(sign) * NX + x)

    def zr_start(s, late):
        for way in range(2):
            zr_copy(s, way, late).start()

    def zr_next(s, late):
        for way in range(2):
            sign = 1 - 2 * way
            t = zz(sign * (4 - s))
            lo = (1 - way if late else way) * zh
            zr_copy(s, way, late).wait_recv()
            zg[t, lo:lo + zh] = zg[t, lo:lo + zh] + zr[way, s + 2 if late else s - 1]
            if s < 4:
                zr_copy(s + 1, way, late).start()

    def x_rows(to):
        return pl.ds(pl.multiple_of(16 * to, 16), 16)

    def zx_start():
        for r in range(1, NX):
            to = (x + r) % NX
            remote(zg.at[z, x_rows(to)], zx.at[r - 1], zx_send, zx_recv, dp, z * NX + to).start()

    def zx_last():
        pltpu.make_async_copy(zx, zx, zx_recv).wait()
        left_ref[2] = zg[z, x_rows(x)] + zx[0] + zx[1] + zx[2]

    def make_perm():
        p = lax.broadcasted_iota(jnp.int32, (NX * T, NX * T), 0)
        q = lax.broadcasted_iota(jnp.int32, (NX * T, NX * T), 1)
        place = ((p // 16) % NZ) * (16 * NX) + (p // T) * 16 + p % 16
        perm[...] = (place == q).astype(F32).astype(BF16)

    def make_table():
        load_owners.wait()
        lane = lax.broadcasted_iota(jnp.int32, (8, T), 1)
        lane_owner = (lane * 43) >> 8
        lane_rank = lane - lane_owner * CAP
        seen = jnp.zeros((8, T), jnp.int32)
        found = jnp.zeros((8, T), jnp.int32)
        mine = jnp.int32(0)
        for b in range(NMP):
            o = own[0, b]
            same = lane_owner == o
            found = jnp.where(same & (seen == lane_rank), b, found)
            seen = seen + same.astype(jnp.int32)
            mine = mine + (o == dp).astype(jnp.int32)
        tabv[...] = (found - mp + NMP) % NMP
        cp = pltpu.make_async_copy(tabv, tab, tab_sem)
        cp.start()
        cp.wait()
        return [jnp.where(k < mine, F32(0), F32(jnp.nan)) for k in range(CAP)]

    def right_out(k, empty):
        lo, n = CHUNK[k]
        r3 = (r3a, r3b)[k]
        for d in range(NT):
            @pl.when(dp != d)
            def _():
                pltpu.make_async_copy(r3.at[d], r3.at[d], r3_recv.at[k, d]).wait()

        first = (RPM * mp + lo) // T
        last = (RPM * mp + lo + n - 1) // T
        row = lax.broadcasted_iota(jnp.int32, (n, T), 0) + (RPM * mp + lo)
        upper = row < last * T
        for g in range(NT):
            one = (g + first) % NT
            two = (g + last) % NT
            for s in range(CAP):
                cut = slice(n * s, n * (s + 1))
                value = jnp.where(upper, r3[one, cut, :], r3[two, cut, :])
                right_ref[s, lo:lo + n, g * T:(g + 1) * T] = value + empty[s]

    def sent_early():
        for i in range(NY):
            @pl.when(has(order[i], other))
            def _():
                ra_copy(i).wait_send()

        @pl.when(has(q2, c))
        def _():
            rb_copy(0, 0).wait_send()
            rb_copy(0, 1).wait_send()

        for way in range(2):
            @pl.when(has((q1, q3)[way], c))
            def _():
                rb_copy(1, way).wait_send()
                rb_copy(2, way).wait_send()

        for l in range(2):
            for step in range(3):
                def done(n):
                    lx_copy(l, step, 0, n).wait_send()
                    lx_copy(l, step, 1, n).wait_send()

                by_parity(x + 4 - l + (0 if step == 0 else 1), done)
        for way in range(2):
            for s in range(1, 5):
                zr_copy(s, way, False).wait_send()
                if s > 1:
                    zr_copy(s, way, True).wait_send()

    def sent_next():
        for i in range(4):
            lz_copy(i).wait_send()
        pltpu.make_async_copy(zx, zx, zx_send).wait()

        @pl.when(active)
        def _():
            for k in range(2):
                sent = (r2a, r2b)[k].at[pl.ds(1, NMP - 1)]
                pltpu.make_async_copy(sent, sent, r2_send.at[k]).wait()
            for i in range(1, NDP):
                r3_copy(0, i).wait_send()

    def sent_late():
        sent = fin.at[pl.ds(1, 19)]
        pltpu.make_async_copy(sent, sent, fin_send).wait()

        @pl.when(active)
        def _():
            for i in range(1, NDP):
                r3_copy(1, i).wait_send()

    for l in (2, 0, 1):
        load_h[l].wait()
        for q in range(4):
            right_part(l, q)
    pl.semaphore_wait(barrier, NMP - 1 + NDP - 1)
    for i in range(4):
        ra_go(i)
    z_part()
    zr_start(1, False)
    zr_start(2, True)
    left_part(0)
    lx_start(0, 0)
    lx_start(0, 1)
    ra_sum(0)
    ra_sum(1)
    ra_sum(2)
    zr_next(1, False)
    left_part(1)
    lx_second(0)
    lx_start(1, 0)
    lx_start(1, 1)
    zr_next(2, True)
    ra_sum(3)
    rb_second()
    zr_next(2, False)
    zr_next(3, True)
    lz_put(0)
    zr_next(3, False)
    lx_second(1)
    empty = make_table()
    make_perm()
    right_whole()
    r2_go(0)
    zr_next(4, True)
    zr_next(4, False)
    zx_start()
    r2_go(1)
    lz_put(1)
    lz_first()
    r3_go(0)
    sent_early()
    r3_go(1)
    zx_last()
    lz_second()
    right_out(0, empty)
    sent_next()
    lz_last()
    right_out(1, empty)
    sent_late()


def per_device(gradient, owners, left_old, right_old):
    rows = gradient.shape[0]
    dma = pltpu.SemaphoreType.DMA
    na, nb = CHUNK[0][1], CHUNK[1][1]
    left_gram, right_gram = pl.pallas_call(
        kernel,
        out_shape=(
            jax.ShapeDtypeStruct((3, 16, 512), F32),
            jax.ShapeDtypeStruct((CAP, RPM, RB), F32),
        ),
        in_specs=[
            pl.BlockSpec(memory_space=pl.ANY),
            pl.BlockSpec(memory_space=pl.ANY),
        ],
        out_specs=(
            pl.BlockSpec(memory_space=pltpu.VMEM),
            pl.BlockSpec(memory_space=pltpu.VMEM),
        ),
        scratch_shapes=[
            pltpu.VMEM((rows, RB), BF16),
            pltpu.VMEM((2, NX, NZ, 16, RB), BF16),
            pltpu.VMEM((NDP, 4, T, T), F32),
            pltpu.VMEM((NY, 4, T, T), F32),
            pltpu.VMEM((2, 2, T, T), F32),
            pltpu.VMEM((2, 4, T, T), F32),
            pltpu.VMEM((RB, T), F32),
            pltpu.VMEM((NMP, RPM, T), F32),
            pltpu.VMEM((NMP, na, T), F32),
            pltpu.VMEM((NMP, nb, T), F32),
            pltpu.VMEM((NDP, CAP * na, T), F32),
            pltpu.VMEM((NDP, CAP * nb, T), F32),
            pltpu.VMEM((NDP, CAP * na, T), F32),
            pltpu.VMEM((NDP, CAP * nb, T), F32),
            pltpu.VMEM((2, 4, 3, T, T), F32),
            pltpu.VMEM((2, 2, 3, T // 2, T), F32),
            pltpu.VMEM((2, 2, 3, T, T), F32),
            pltpu.VMEM((NZ, 4, 2, 16, T), F32),
            pltpu.VMEM((2, 4, 2, 16, T), F32),
            pltpu.VMEM((2, 2, 2, 16, T), F32),
            pltpu.VMEM((20, 2, 16, T), F32),
            pltpu.VMEM((NZ, 16 * NX, NX * T), F32),
            pltpu.VMEM((2, 7, 8 * NX, NX * T), F32),
            pltpu.VMEM((3, 16, NX * T), F32),
            pltpu.VMEM((4 * T, 4 * T), BF16),
            pltpu.SMEM((1, NMP), jnp.int32),
            pltpu.VMEM((8, T), jnp.int32),
            pltpu.SMEM((8, T), jnp.int32),
            dma((4,)), dma,
            dma((NY,)), dma((NY,)), dma((6,)), dma((6,)),
            dma((2,)), dma((2,)), dma((2, NDP)), dma((2, NDP)),
            dma((2, 6)), dma((2, 6)), dma((4,)), dma((4,)), dma, dma,
            dma((2, 7)), dma((2, 7)), dma, dma,
        ],
        compiler_params=pltpu.CompilerParams(
            collective_id=0, has_side_effects=True, vmem_limit_bytes=105 * 512 * 1024
        ),
        name="stats",
    )(gradient, owners.reshape(1, NMP))
    left_stats = BETA * left_old + left_gram
    right_stats = jnp.where(jnp.isnan(right_gram), 0.0, BETA * right_old + right_gram)
    return left_stats, right_stats


def solution(mesh):
    in_specs = (P("dp", "mp"), P(), P("dp", "mp", None), P("dp", "mp", None))
    out_specs = (P("dp", "mp", None), P("dp", "mp", None))
    return jax.shard_map(
        per_device, mesh=mesh, in_specs=in_specs, out_specs=out_specs, check_vma=False
    )
```
